32 devices in a mesh: gx: 8 (over z, x), gy: 4 (over y, core).
Axes of the slice: x: 2, y: 2, z: 4, core: 2. Of those that a mesh axis runs over, the one named last changes fastest.
Arguments:
- velocity: float32 [3, 256, 4, 512], P(None, 'gx', None, 'gy'), may hold values from -6 to 6
- pair_blocks: float32 [8, 4, 256, 128], P('gx', 'gy'), may hold values from 0.1 to 2
- send_up: int32 [8, 4, 128], P('gx', 'gy'), may hold values from 0 to 255
- send_side: int32 [8, 4, 2, 64], P('gx', 'gy'), may hold values from 0 to 255
- send_diag: int32 [8, 4, 2, 32], P('gx', 'gy'), may hold values from 0 to 255
- depart_tile: int32 [8, 4, 2, 256], P('gx', 'gy'), may hold values from 0 to 5, as said below
- depart_slot: int32 [8, 4, 2, 256], P('gx', 'gy'), may hold values from 0 to 255, as said below
- interp_weights: bfloat16 [8, 4, 256, 64, 128], P('gx', 'gy'), may hold values from 0 to 1, as said below
Outputs:
- pair_next: float32 [8, 4, 256, 128], P('gx', 'gy')
The draws below stay inside these ranges and needn't reach their ends.
Inputs may be any that keep to these rules, and one draw needn't show every extreme that they name: `depart_tile`: 0 is the own tile, 1 the upstream tile along gx, 2 the spanwise neighbour at lower gy, 3 the one at higher gy, 4 and 5 the upstream tile's neighbours at lower and higher gy. `depart_slot`: below 256 for tile 0, 128 for tile 1, 64 for tiles 2 and 3, 32 for tiles 4 and 5; each bound minus one is reached. `interp_weights`: the 128 columns are the cells of the two departure blocks taken as a 4 x 4 x 8 box; each cell's row holds the eight trilinear weights of one point inside that box, summing to one, and zeros elsewhere.
All inputs are finite; a program needn't handle non-finite values.
Results may differ from the reference program's by a relative error of at most 0.0003.
Values sent between devices are 32-bit elements; how exact they have to be, the bound alone decides.
No kernel may reach another device: no remote copies, remote signals or barrier semaphores. Data moves between devices by JAX's collectives and lax.ppermute only.
A program may use at most 64 MiB of HBM per device.

```python
import jax
import jax.numpy as jnp
from jax import lax

CX = 32
CY = 128
LZ = 4
NBD = 256
CAPX = 128
CAPY = 64
CAPD = 32
NX = 256
NY = 512
N_GX = 8
N_GY = 4


def departure_draw(key):
    key = jax.random.fold_in(key, 11)
    tile_key, slot_key = jax.random.split(key)
    shape = (N_GX, N_GY, 2, NBD)
    choose = jax.random.randint(tile_key, shape, 0, 10)
    table = jnp.array([0, 0, 0, 1, 1, 1, 2, 3, 4, 5], jnp.int32)
    tile_ids = table[choose]
    limits = jnp.array([NBD, CAPX, CAPY, CAPY, CAPD, CAPD], jnp.int32)
    slot_ids = jax.random.randint(slot_key, shape, 0, limits[tile_ids])
    return (tile_ids.astype(jnp.int32), slot_ids.astype(jnp.int32))


def draw_depart_tile(key, part):
    return departure_draw(key)[0]


def draw_depart_slot(key, part):
    return departure_draw(key)[1]


def linear_pair(index, base, fraction):
    return jnp.where(index == base, 1.0 - fraction, 0.0) + jnp.where(index == base + 1, fraction, 0.0)


def draw_interp_weights(key, part):
    key = jax.random.fold_in(key, 23)
    keys = jax.random.split(key, 6)
    shape = (N_GX, N_GY, NBD, 64, 1)
    base_x = jax.random.randint(keys[0], shape, 0, 3)
    base_z = jax.random.randint(keys[1], shape, 0, 3)
    base_y = jax.random.randint(keys[2], shape, 0, 7)
    frac_x = jax.random.uniform(keys[3], shape, jnp.float32)
    frac_z = jax.random.uniform(keys[4], shape, jnp.float32)
    frac_y = jax.random.uniform(keys[5], shape, jnp.float32)
    column = jnp.arange(128, dtype=jnp.int32)
    weight_x = linear_pair(column // 32, base_x, frac_x)
    weight_z = linear_pair(column // 8 % 4, base_z, frac_z)
    weight_y = linear_pair(column % 8, base_y, frac_y)
    return (weight_x * weight_z * weight_y).astype(jnp.float32).astype(jnp.bfloat16)


def touch_ends(result, stream_key, least, top_value):
    extent = result.shape
    place = [jax.random.randint(jax.random.fold_in(stream_key, axis), (), 0, extent[axis]) for axis in range(len(extent))]
    result = result.at[tuple(place)].set(least)
    longest = extent.index(max(extent))
    place[longest] = (place[longest] + 1) % extent[longest]
    return result.at[tuple(place)].set(top_value)


def shard_levels(stream_key, extent, shards, low, largest):
    gain, own = 1.0, jax.random.fold_in(stream_key, 6)
    for axis_at, parts in shards:
        draws = jnp.exp(jax.random.uniform(jax.random.fold_in(own, axis_at), (parts,), jnp.float32, low / len(shards), largest / len(shards)))
        gain = gain * jnp.repeat(draws, extent[axis_at] // parts).reshape([-1 if axis == axis_at else 1 for axis in range(len(extent))])
    return gain


def scatter_about(own_key, extent, deviation, limit, pieces=(), kind=jnp.bfloat16):
    values = deviation * jax.random.normal(own_key, extent, jnp.float32)
    if pieces:
        values = values * shard_levels(own_key, extent, pieces, -0.22, 0.18)
    return jnp.clip(values, -limit, limit).astype(kind)


def setup_inputs(seed: int = 0) -> dict:
    key_of = jax.random.split(jax.random.key(seed), 9)
    return {
        "velocity": scatter_about(key_of[0], (3, NX, LZ, NY), 1.0, 6.0, ((1, 8), (3, 4)), jnp.float32),
        "pair_blocks": jnp.clip(0.1 + 1.9 * jax.random.uniform(key_of[1], (N_GX, N_GY, NBD, 128), jnp.float32) ** shard_levels(key_of[1], (N_GX, N_GY, NBD, 128), ((0, 8), (1, 4)), -0.2, 0.2), 0.1, 2.0),
        "send_up": touch_ends(jax.random.randint(key_of[2], (N_GX, N_GY, CAPX), 0, NBD), jax.random.fold_in(key_of[2], 1), 0, NBD - 1).astype(jnp.int32),
        "send_side": touch_ends(jax.random.randint(key_of[3], (N_GX, N_GY, 2, CAPY), 0, NBD), jax.random.fold_in(key_of[3], 1), 0, NBD - 1).astype(jnp.int32),
        "send_diag": touch_ends(jax.random.randint(key_of[4], (N_GX, N_GY, 2, CAPD), 0, NBD), jax.random.fold_in(key_of[4], 1), 0, NBD - 1).astype(jnp.int32),
        "depart_tile": draw_depart_tile(jax.random.fold_in(key_of[8], 71), 0),
        "depart_slot": draw_depart_slot(jax.random.fold_in(key_of[8], 71), 0),
        "interp_weights": draw_interp_weights(jax.random.fold_in(key_of[8], 71), 0),
    }


time_step = 0.5

def vertical_diff(field):
    return jnp.concatenate([field[:, :, 1:2] - field[:, :, 0:1], (field[:, :, 2:] - field[:, :, :-2]) * 0.5, field[:, :, -1:] - field[:, :, -2:-1]], axis=2)

def strain_parts(field):
    along_x = (field[:, 2:, :, 1:-1] - field[:, :-2, :, 1:-1]) * 0.5
    along_y = (field[:, 1:-1, :, 2:] - field[:, 1:-1, :, :-2]) * 0.5
    along_z = vertical_diff(field[:, 1:-1, :, 1:-1])
    gradient = jnp.stack([along_x, along_y, along_z], axis=1)
    strain_rate = 0.5 * (gradient + jnp.swapaxes(gradient, 0, 1))
    magnitude = jnp.sqrt(2.0 * lax.optimization_barrier(jnp.sum(strain_rate * strain_rate, axis=(0, 1))))
    return (strain_rate, magnitude)

def test_filter(field):
    across = 0.25 * field[..., :-2, :, :] + 0.5 * field[..., 1:-1, :, :] + 0.25 * field[..., 2:, :, :]
    return 0.25 * across[..., :-2] + 0.5 * across[..., 1:-1] + 0.25 * across[..., 2:]

def model_terms(extended):
    strain_rate, magnitude = strain_parts(extended)
    filtered_product = test_filter(magnitude * strain_rate)
    smooth = test_filter(extended)
    strain_test, magnitude_test = strain_parts(smooth)
    model_tensor = 2.0 * (filtered_product - 4.0 * magnitude_test * strain_test)
    center = extended[:, 1:-1, :, 1:-1]
    smooth_center = smooth[:, 1:-1, :, 1:-1]
    leonard = test_filter(center[:, None] * center[None, :]) - smooth_center[:, None] * smooth_center[None, :]
    return (lax.optimization_barrier(jnp.sum(leonard * model_tensor, axis=(0, 1))), lax.optimization_barrier(jnp.sum(model_tensor * model_tensor, axis=(0, 1))))

def slot_offsets(tile_ids):
    starts = jnp.array([0, NBD, NBD + CAPX, NBD + CAPX + CAPY, NBD + CAPX + 2 * CAPY, NBD + CAPX + 2 * CAPY + CAPD], jnp.int32)
    match = tile_ids[..., None] == jnp.arange(6, dtype=jnp.int32)
    return lax.optimization_barrier(jnp.sum(jnp.where(match, starts, 0), axis=-1)).astype(jnp.int32)

def departure_update(weights, first, second, lm_blocks, mm_blocks):
    lm_rows = jnp.concatenate([first[..., :64], second[..., :64]], axis=-1)
    mm_rows = jnp.concatenate([first[..., 64:], second[..., 64:]], axis=-1)
    stacked = jnp.stack([lm_rows, mm_rows], axis=-2)
    departed = jnp.einsum('...kij,...kcj->...kci', weights.astype(jnp.float32), stacked, precision=lax.Precision.HIGHEST)
    lm_depart = departed[..., 0, :]
    mm_depart = departed[..., 1, :]
    timescale = 1.5 * (lm_depart * mm_depart) ** (-0.125)
    ratio = time_step / timescale
    weight_new = ratio / (1.0 + ratio)
    lm_next = jnp.maximum(weight_new * lm_blocks + (1.0 - weight_new) * lm_depart, 0.0)
    mm_next = weight_new * mm_blocks + (1.0 - weight_new) * mm_depart
    return jnp.concatenate([lm_next, mm_next], axis=-1)

def pick_rows(field, lists):
    return jnp.take_along_axis(field, lists[:, :, :, None], axis=2)

def reference(velocity, pair_blocks, send_up, send_side, send_diag, depart_tile, depart_slot, interp_weights):
    extended = jnp.pad(velocity, ((0, 0), (2, 2), (0, 0), (2, 2)), mode='wrap')
    lm_field, mm_field = model_terms(extended)
    lm_blocks = lm_field.reshape(N_GX, CX, LZ, N_GY, CY).transpose(0, 3, 1, 2, 4).reshape(N_GX, N_GY, NBD, 64)
    mm_blocks = mm_field.reshape(N_GX, CX, LZ, N_GY, CY).transpose(0, 3, 1, 2, 4).reshape(N_GX, N_GY, NBD, 64)
    from_up = pick_rows(jnp.roll(pair_blocks, 1, 0), jnp.roll(send_up, 1, 0))
    from_low = pick_rows(jnp.roll(pair_blocks, 1, 1), jnp.roll(send_side, 1, 1)[:, :, 0])
    from_high = pick_rows(jnp.roll(pair_blocks, -1, 1), jnp.roll(send_side, -1, 1)[:, :, 1])
    corner = jnp.roll(pair_blocks, 1, 0)
    corner_lists = jnp.roll(send_diag, 1, 0)
    diag_low = pick_rows(jnp.roll(corner, 1, 1), jnp.roll(corner_lists, 1, 1)[:, :, 0])
    diag_high = pick_rows(jnp.roll(corner, -1, 1), jnp.roll(corner_lists, -1, 1)[:, :, 1])
    candidates = jnp.concatenate([pair_blocks, from_up, from_low, from_high, diag_low, diag_high], axis=2)
    pool_index = (slot_offsets(depart_tile) + depart_slot).astype(jnp.int32)
    sources = pick_rows(candidates, pool_index.reshape(N_GX, N_GY, 2 * NBD)).reshape(N_GX, N_GY, 2, NBD, 128)

    def one_column(items):
        return departure_update(items[0], items[1], items[2], items[3], items[4])
    return lax.map(one_column, (interp_weights, sources[:, :, 0], sources[:, :, 1], lm_blocks, mm_blocks))
```

```python
import functools

import jax
import jax.numpy as jnp
from jax import lax
from jax.experimental import pallas as pl
from jax.experimental.pallas import tpu as pltpu
from jax.sharding import PartitionSpec as P

CX = 32
LZ = 4
NBD = 256
CAPX = 128
CAPY = 64
CAPD = 32

TIME_STEP = 0.5

VEL_AT = CAPD
DIAG1_AT = CAPD + 24
UP_AT = 2 * CAPD + 24
X_ROWS = UP_AT + CAPX
Y_ROWS = CAPY + CX
R_ROWS = CAPD + 8

POOL = NBD + CAPX + 2 * CAPY + 2 * CAPD
POOL_PAD = 640
UP_POOL = NBD
LOW_POOL = NBD + CAPX
HIGH_POOL = LOW_POOL + CAPY
DIAG_LOW_POOL = HIGH_POOL + CAPY
DIAG_HIGH_POOL = DIAG_LOW_POOL + CAPD

EXT = 48
F32 = jnp.float32
BF16 = jnp.bfloat16


def lanes_of(shape):
    return lax.broadcasted_iota(jnp.int32, shape, 1)


def roll_lanes(x, shift):
    shift = shift % 128
    return x if shift == 0 else pltpu.roll(x, shift, 1)


def odd(axis):
    return lax.rem(lax.axis_index(axis), 2) == 1


def pack_x_kernel(up_list, diag_list, rows, vel, s0, t0):
    is_odd = odd("gx")

    def gather(out):
        for i in range(CAPD):
            out[i : i + 1, :] = rows[pl.ds(diag_list[0, i], 1), :]
            out[DIAG1_AT + i : DIAG1_AT + i + 1, :] = rows[pl.ds(diag_list[1, i], 1), :]
        for i in range(CAPX):
            out[UP_AT + i : UP_AT + i + 1, :] = rows[pl.ds(up_list[i], 1), :]

    def edge(out, at):
        for c in range(3):
            out[VEL_AT + 8 * c : VEL_AT + 8 * c + 8, :] = vel[c * 128 + at : c * 128 + at + 8, :]

    @pl.when(is_odd)
    def _():
        gather(s0)
        edge(s0, 120)
        edge(t0, 0)

    @pl.when(jnp.logical_not(is_odd))
    def _():
        gather(t0)
        edge(t0, 120)
        edge(s0, 0)


def pack_y_kernel(side_list, rows, vel, y1, y0):
    is_odd = odd("gy")
    first = jnp.where(is_odd, 0, 1)
    for i in range(CAPY):
        y1[i : i + 1, :] = rows[pl.ds(side_list[first, i], 1), :]
        y0[i : i + 1, :] = rows[pl.ds(side_list[1 - first, i], 1), :]
    lane = lanes_of((8, 128))
    for xv in range(4):
        plus = jnp.zeros((8, 128), F32)
        minus = jnp.zeros((8, 128), F32)
        for z in range(LZ):
            for c in range(3):
                base = z * 32 + c * 8
                plane = vel[pl.ds(c * 128 + xv * 32 + z, 8, stride=4), :]
                here = (lane >= base) & (lane < base + 2)
                plus = jnp.where(here, roll_lanes(plane, base - 126), plus)
                minus = jnp.where(here, roll_lanes(plane, base), minus)
        at = CAPY + 8 * xv
        y1[at : at + 8, :] = jnp.where(is_odd, plus, minus)
        y0[at : at + 8, :] = jnp.where(is_odd, minus, plus)


def relay_kernel(s0, t0, ry1, ry0):
    x_odd = odd("gx")
    y_odd = odd("gy")

    def upper(at):
        return jnp.where(x_odd, t0[at : at + 8, :], s0[at : at + 8, :])

    def lower(at):
        return jnp.where(x_odd, s0[at : at + 8, :], t0[at : at + 8, :])

    for i in range(0, CAPD, 8):
        plus, minus = upper(i), upper(DIAG1_AT + i)
        ry1[i : i + 8, :] = jnp.where(y_odd, plus, minus)
        ry0[i : i + 8, :] = jnp.where(y_odd, minus, plus)
    lane = lanes_of((8, 128))
    plus = jnp.zeros((8, 128), F32)
    minus = jnp.zeros((8, 128), F32)
    for c in range(3):
        for k, part in enumerate((upper(VEL_AT + 8 * c), lower(VEL_AT + 8 * c))):
            base = (2 * c + k) * 8
            here = (lane >= base) & (lane < base + 2)
            plus = jnp.where(here, roll_lanes(part, base - 126), plus)
            minus = jnp.where(here, roll_lanes(part, base), minus)
    ry1[CAPD:, :] = jnp.where(y_odd, plus, minus)
    ry0[CAPD:, :] = jnp.where(y_odd, minus, plus)


PAIRS = ((0, 0), (1, 1), (2, 2), (0, 1), (0, 2), (1, 2))


def plane_diff(f):
    last = len(f) - 1
    return [
        f[1] - f[0]
        if p == 0
        else f[last] - f[last - 1]
        if p == last
        else (f[p + 1] - f[p - 1]) * 0.5
        for p in range(last + 1)
    ]


def strip_diff(f):
    (f,) = f
    level = lanes_of(f.shape) // 32
    above, below = roll_lanes(f, -32), roll_lanes(f, 32)
    inner = (above - below) * 0.5
    return [jnp.where(level == 0, above - f, jnp.where(level == LZ - 1, f - below, inner))]


def strain(before, here, after, along_z):
    grad = [
        (
            (after[i] - before[i]) * 0.5,
            (roll_lanes(here[i], -1) - roll_lanes(here[i], 1)) * 0.5,
            along_z[i],
        )
        for i in range(3)
    ]
    rate = [grad[i][j] if i == j else 0.5 * (grad[i][j] + grad[j][i]) for i, j in PAIRS]
    own = rate[0] * rate[0] + rate[1] * rate[1] + rate[2] * rate[2]
    cross = rate[3] * rate[3] + rate[4] * rate[4] + rate[5] * rate[5]
    return rate, jnp.sqrt(2.0 * own + 4.0 * cross)


def filtered(before, here, after):
    across = 0.25 * (before + after) + 0.5 * here
    return 0.25 * (roll_lanes(across, 1) + roll_lanes(across, -1)) + 0.5 * across


def stencil(u, q, planes, diff, emit):
    for r in range(0, CX + 8, 8):
        here = [[u[c, p, r + 1 : r + 9, :] for p in range(planes)] for c in range(3)]
        along_z = [diff(here[c]) for c in range(3)]
        for p in range(planes):
            before = [u[c, p, r : r + 8, :] for c in range(3)]
            after = [u[c, p, r + 2 : r + 10, :] for c in range(3)]
            mid = [here[c][p] for c in range(3)]
            rate, size = strain(before, mid, after, [along_z[c][p] for c in range(3)])
            for n, (i, j) in enumerate(PAIRS):
                q[n, p, r : r + 8, :] = size * rate[n]
                q[6 + n, p, r : r + 8, :] = mid[i] * mid[j]
            for c in range(3):
                q[12 + c, p, r : r + 8, :] = filtered(before[c], mid[c], after[c])
    for r in range(0, CX, 8):
        here = [[q[12 + c, p, r + 1 : r + 9, :] for p in range(planes)] for c in range(3)]
        along_z = [diff(here[c]) for c in range(3)]
        for p in range(planes):
            before = [q[12 + c, p, r : r + 8, :] for c in range(3)]
            after = [q[12 + c, p, r + 2 : r + 10, :] for c in range(3)]
            mid = [here[c][p] for c in range(3)]
            rate, size = strain(before, mid, after, [along_z[c][p] for c in range(3)])
            size = 4.0 * size

            def smoothed(n):
                return filtered(
                    q[n, p, r : r + 8, :], q[n, p, r + 1 : r + 9, :], q[n, p, r + 2 : r + 10, :]
                )

            lm, mm = 0.0, 0.0
            for n, (i, j) in enumerate(PAIRS):
                model = 2.0 * (smoothed(n) - size * rate[n])
                leonard = smoothed(6 + n) - mid[i] * mid[j]
                weight = 1.0 if i == j else 2.0
                lm += weight * (leonard * model)
                mm += weight * (model * model)
            emit(p, r, lm, mm)


def main_kernel(
    vel, s0, t0, y1, y0, tiles, slots, weights, lm, mm, strips, picks, held, u, q, sem
):
    fetch = pltpu.make_async_copy(weights, held, sem)
    fetch.start()
    x_odd, y_odd = odd("gx"), odd("gy")
    lane = lanes_of((8, 128))
    for c in range(3):
        for z in range(LZ):
            at = VEL_AT + 8 * c + z
            s_rows = s0[pl.ds(at, 2, stride=4), :]
            t_rows = t0[pl.ds(at, 2, stride=4), :]
            u[c, z, 0:2, :] = jnp.where(x_odd, t_rows, s_rows)
            u[c, z, 2 : CX + 2, :] = vel[pl.ds(c * 128 + z, CX, stride=4), :]
            u[c, z, CX + 2 : CX + 4, :] = jnp.where(x_odd, s_rows, t_rows)
    for c in range(3):
        for r in range(0, CX + 8, 8):
            strip = jnp.zeros((8, 128), F32)
            for z in range(LZ):
                base = 32 * z
                plane = u[c, z, r : r + 8, :]
                left = (lane >= base + 2) & (lane < base + 6)
                right = (lane >= base + 16) & (lane < base + 20)
                strip = jnp.where(left, roll_lanes(plane, base + 2), strip)
                strip = jnp.where(right, roll_lanes(plane, base + 16 - 124), strip)
            strips[c, r : r + 8, :] = strip
        for r in range(0, CX, 8):
            at = CAPY + r
            low = jnp.where(y_odd, y0[at : at + 8, :], y1[at : at + 8, :])
            high = jnp.where(y_odd, y1[at : at + 8, :], y0[at : at + 8, :])
            strip = strips[c, r + 2 : r + 10, :]
            strip = jnp.where(lane % 32 < 2, roll_lanes(low, -8 * c), strip)
            here = (lane % 32 >= 20) & (lane % 32 < 22)
            strip = jnp.where(here, roll_lanes(high, 20 - 8 * c), strip)
            strips[c, r + 2 : r + 10, :] = strip

    def emit(z, r, lm_part, mm_part):
        for k in range(2):
            lm[pl.ds(8 * r + 2 * z + k, 8, stride=8), :] = lm_part
            mm[pl.ds(8 * r + 2 * z + k, 8, stride=8), :] = mm_part

    stencil(u, q, LZ, plane_diff, emit)

    tile = tiles[...]
    starts = (0, UP_POOL, LOW_POOL, HIGH_POOL, DIAG_LOW_POOL, DIAG_HIGH_POOL)
    index = slots[...]
    for n, start in enumerate(starts):
        index = index + jnp.where(tile == n, start, 0)
    index = index.astype(F32)
    column = lanes_of((128, 128)).astype(F32)
    for k in range(2):
        for half in range(2):
            line = index[k : k + 1, half * 128 : half * 128 + 128]
            wanted = jnp.transpose(jnp.broadcast_to(line, (128, 128)))
            for part in range(POOL_PAD // 128):
                hit = wanted == column + 128.0 * part
                at = k * NBD + half * 128
                picks[at : at + 128, part * 128 : part * 128 + 128] = jnp.where(
                    hit, 1.0, 0.0
                ).astype(BF16)
    fetch.wait()


def final_kernel(
    lm_in, mm_in, strips, ry1, ry0, s0, t0, y1, y0, rows, picks, weights, out,
    u, q, lm, mm, pool, picked,
):
    x_odd, y_odd = odd("gx"), odd("gy")
    lane = lanes_of((8, 128))
    lm[...] = lm_in[...]
    mm[...] = mm_in[...]

    def candidates(at, value):
        high = value.astype(BF16)
        size = value.shape[0]
        pool[at : at + size, 0:128] = high
        pool[at : at + size, 128:256] = (value - high.astype(F32)).astype(BF16)

    candidates(0, rows[...])
    candidates(UP_POOL, jnp.where(x_odd, t0[UP_AT:, :], s0[UP_AT:, :]))
    candidates(LOW_POOL, jnp.where(y_odd, y0[:CAPY, :], y1[:CAPY, :]))
    candidates(HIGH_POOL, jnp.where(y_odd, y1[:CAPY, :], y0[:CAPY, :]))
    candidates(DIAG_LOW_POOL, jnp.where(y_odd, ry0[:CAPD, :], ry1[:CAPD, :]))
    candidates(DIAG_HIGH_POOL, jnp.where(y_odd, ry1[:CAPD, :], ry0[:CAPD, :]))
    pool[POOL:, :] = jnp.zeros((POOL_PAD - POOL, 256), BF16)
    picked[...] = jnp.dot(picks[...], pool[...], preferred_element_type=F32)

    low = jnp.where(y_odd, ry0[CAPD:, :], ry1[CAPD:, :])
    high = jnp.where(y_odd, ry1[CAPD:, :], ry0[CAPD:, :])
    level = lane // 32
    u[...] = strips[...].reshape(u.shape)
    for c in range(3):
        for k, at in enumerate((0, CX + 2)):
            base = (2 * c + k) * 8
            for x in range(2):
                row = u[c, 0, at + x : at + x + 1, :]
                one = lanes_of((1, 128))
                for z in range(LZ):
                    line = low[4 * x + z : 4 * x + z + 1, :]
                    here = (one >= 32 * z) & (one < 32 * z + 2)
                    row = jnp.where(here, roll_lanes(line, 32 * z - base), row)
                    line = high[4 * x + z : 4 * x + z + 1, :]
                    here = (one >= 32 * z + 20) & (one < 32 * z + 22)
                    row = jnp.where(here, roll_lanes(line, 32 * z + 20 - base), row)
                u[c, 0, at + x : at + x + 1, :] = row
    del level

    def emit(_, r, lm_part, mm_part):
        for into, part in ((lm, lm_part), (mm, mm_part)):
            for z in range(LZ):
                left = roll_lanes(part, -(32 * z + 2))
                right = roll_lanes(part, 126 - (32 * z + 18))
                for k in range(2):
                    at = pl.ds(8 * r + 2 * z + k, 8, stride=8)
                    value = jnp.where(lane < 2, left, jnp.where(lane >= 126, right, into[at, :]))
                    into[at, :] = value

    stencil(u, q, 1, strip_diff, emit)

    row_of = lax.broadcasted_iota(jnp.int32, (8, 128), 0)
    front = lane < 64
    even = row_of % 2 == 0
    for x in range(CX):
        terms = []
        for half in range(2):
            first = picked[8 * x : 8 * x + 8, 128 * half : 128 * half + 128]
            second = picked[NBD + 8 * x : NBD + 8 * x + 8, 128 * half : 128 * half + 128]
            terms.append(jnp.where(front, first, roll_lanes(second, 64)))
            terms.append(jnp.where(front, roll_lanes(first, 64), second))
        left = jnp.concatenate(terms, axis=0).astype(BF16)
        product = lax.dot_general(
            left,
            weights[512 * x : 512 * x + 512, :],
            (((1,), (1,)), ((), ())),
            preferred_element_type=F32,
        )
        product = product[:16] + product[16:]
        found = []
        for at in (0, 8):
            merged = product[at : at + 8, 384:512]
            for part in (2, 1, 0):
                mine = row_of // 2 == part
                merged = jnp.where(mine, product[at : at + 8, 128 * part : 128 * part + 128], merged)
            found.append(merged)
        lm_depart, mm_depart = found
        lm_block, mm_block = lm[8 * x : 8 * x + 8, :], mm[8 * x : 8 * x + 8, :]
        ratio = (TIME_STEP / 1.5) * jnp.exp(0.125 * jnp.log(lm_depart * mm_depart))
        weight = ratio / (1.0 + ratio)
        lm_next = jnp.maximum(weight * lm_block + (1.0 - weight) * lm_depart, 0.0)
        mm_next = weight * mm_block + (1.0 - weight) * mm_depart
        lm_next = jnp.where(even, lm_next, roll_lanes(lm_next, 64))
        mm_next = jnp.where(even, roll_lanes(mm_next, 64), mm_next)
        out[8 * x : 8 * x + 8, :] = jnp.where(front, lm_next, mm_next)


def vmem(count=1):
    return [pl.BlockSpec(memory_space=pltpu.VMEM)] * count


def smem(count=1):
    return [pl.BlockSpec(memory_space=pltpu.SMEM)] * count


def array(*shape, dtype=F32):
    return jax.ShapeDtypeStruct(shape, dtype)


def call(kernel, ins, outs, scratch=(), flops=1000):
    return pl.pallas_call(
        kernel,
        in_specs=ins,
        out_specs=tuple(vmem(len(outs))) if isinstance(outs, tuple) else vmem()[0],
        out_shape=outs,
        scratch_shapes=list(scratch),
        compiler_params=pltpu.CompilerParams(vmem_limit_bytes=32 * 1024 * 1024),
        cost_estimate=pl.CostEstimate(flops=flops, bytes_accessed=flops, transcendentals=0),
    )


def swap(block, axis, start):
    count = lax.axis_size(axis)
    ahead = [(i, (i + 1) % count) for i in range(start, count, 2)]
    return lax.ppermute(block, axis, ahead + [(j, i) for i, j in ahead])


def on_device(
    velocity, pair_blocks, send_up, send_side, send_diag, depart_tile, depart_slot, interp_weights
):
    vel = velocity.reshape(3 * CX * LZ, 128)
    rows = pair_blocks[0, 0]
    weights = interp_weights.reshape(NBD * 64, 128)

    s0, t0 = call(pack_x_kernel, smem(2) + vmem(2), (array(X_ROWS, 128),) * 2)(
        send_up[0, 0], send_diag[0, 0], rows, vel
    )
    s0 = swap(s0, "gx", 1)
    t0 = swap(t0, "gx", 0)
    y1, y0 = call(pack_y_kernel, smem(1) + vmem(2), (array(Y_ROWS, 128),) * 2)(
        send_side[0, 0], rows, vel
    )
    y1 = swap(y1, "gy", 1)
    y0 = swap(y0, "gy", 0)
    ry1, ry0 = call(relay_kernel, vmem(2), (array(R_ROWS, 128),) * 2)(s0, t0)
    ry1 = swap(ry1, "gy", 1)
    ry0 = swap(ry0, "gy", 0)
    lm, mm, strips, picks, held = call(
        main_kernel,
        vmem(7) + [pl.BlockSpec(memory_space=pl.ANY)],
        (
            array(NBD, 128),
            array(NBD, 128),
            array(3, EXT, 128),
            array(2 * NBD, POOL_PAD, dtype=BF16),
            array(NBD * 64, 128, dtype=BF16),
        ),
        [
            pltpu.VMEM((3, LZ, EXT, 128), F32),
            pltpu.VMEM((15, LZ, EXT, 128), F32),
            pltpu.SemaphoreType.DMA,
        ],
        flops=4000000,
    )(vel, s0, t0, y1, y0, depart_tile[0, 0], depart_slot[0, 0], weights)
    result = call(
        final_kernel,
        vmem(12),
        array(NBD, 128),
        [
            pltpu.VMEM((3, 1, EXT, 128), F32),
            pltpu.VMEM((15, 1, EXT, 128), F32),
            pltpu.VMEM((NBD, 128), F32),
            pltpu.VMEM((NBD, 128), F32),
            pltpu.VMEM((POOL_PAD, 256), BF16),
            pltpu.VMEM((2 * NBD, 256), F32),
        ],
    )(lm, mm, strips, ry1, ry0, s0, t0, y1, y0, rows, picks, held)
    return result[None, None]


def solution(mesh):
    return jax.shard_map(
        on_device,
        mesh=mesh,
        in_specs=(
            P(None, "gx", None, "gy"),
            P("gx", "gy", None, None),
            P("gx", "gy", None),
            P("gx", "gy", None, None),
            P("gx", "gy", None, None),
            P("gx", "gy", None, None),
            P("gx", "gy", None, None),
            P("gx", "gy", None, None, None),
        ),
        out_specs=P("gx", "gy", None, None),
        check_vma=False,
    )
```

```python
import functools

import jax
import jax.numpy as jnp
from jax import lax
from jax.experimental import pallas as pl
from jax.experimental.pallas import tpu as pltpu
from jax.sharding import PartitionSpec as P

CX = 32
LZ = 4
NBD = 256
CAPX = 128
CAPY = 64
CAPD = 32

TIME_STEP = 0.5

VEL_AT = CAPD
DIAG1_AT = CAPD + 24
UP_AT = 2 * CAPD + 24
X_ROWS = UP_AT + CAPX
BACK_ROWS = 24
Y_ROWS = CAPY + CX
R_ROWS = CAPD + 8

POOL = NBD + CAPX + 2 * CAPY
POOL_DIAG = 128
UP_POOL = NBD
LOW_POOL = NBD + CAPX
HIGH_POOL = LOW_POOL + CAPY
DIAG_LOW_POOL = HIGH_POOL + CAPY
DIAG_HIGH_POOL = DIAG_LOW_POOL + CAPD

EXT = 48
GROUP = 8 * 64
EARLY = 12
SECOND = 10
F32 = jnp.float32
BF16 = jnp.bfloat16


def lanes_of(shape):
    return lax.broadcasted_iota(jnp.int32, shape, 1)


def roll_lanes(x, shift):
    shift = shift % 128
    return x if shift == 0 else pltpu.roll(x, shift, 1)


def odd(axis):
    return lax.rem(lax.axis_index(axis), 2) == 1


def pack_x_kernel(
    up_hbm, diag_hbm, rows_hbm, vel_hbm, ahead, rows, vel, up_list, diag_list, sems
):
    fetches = [
        pltpu.make_async_copy(source, target, sems.at[n])
        for n, (source, target) in enumerate(
            ((up_hbm, up_list), (diag_hbm, diag_list), (rows_hbm, rows), (vel_hbm, vel))
        )
    ]
    for fetch in fetches:
        fetch.start()
    for fetch in fetches[:3]:
        fetch.wait()
    for i in range(CAPD):
        ahead[i : i + 1, :] = rows[pl.ds(diag_list[0, i], 1), :]
        ahead[DIAG1_AT + i : DIAG1_AT + i + 1, :] = rows[pl.ds(diag_list[1, i], 1), :]
    for i in range(CAPX):
        ahead[UP_AT + i : UP_AT + i + 1, :] = rows[pl.ds(up_list[i], 1), :]
    fetches[3].wait()
    for c in range(3):
        ahead[VEL_AT + 8 * c : VEL_AT + 8 * c + 8, :] = vel[c * 128 + 120 : c * 128 + 128, :]


def weight_copy(weights, start, held, sem):
    return pltpu.make_async_copy(
        weights.at[pl.ds(start * GROUP, held.shape[0]), :], held, sem
    )


def pack_y(sources, outs, side_list, sems, weight_copies):
    side_hbm, tiles_hbm, slots_hbm, rows, vel = sources
    y1, y0, tiles, slots = outs
    is_odd = odd("gy")
    first = jnp.where(is_odd, 0, 1)
    fetches = [
        pltpu.make_async_copy(source, target, sems.at[n])
        for n, (source, target) in enumerate(
            ((side_hbm, side_list), (tiles_hbm, tiles), (slots_hbm, slots))
        )
    ]
    fetches += weight_copies
    for fetch in fetches:
        fetch.start()
    fetches[0].wait()
    for i in range(CAPY):
        y1[i : i + 1, :] = rows[pl.ds(side_list[first, i], 1), :]
        y0[i : i + 1, :] = rows[pl.ds(side_list[1 - first, i], 1), :]
    lane = lanes_of((8, 128))
    for xv in range(4):
        plus = jnp.zeros((8, 128), F32)
        minus = jnp.zeros((8, 128), F32)
        for z in range(LZ):
            for c in range(3):
                base = z * 32 + c * 8
                plane = vel[pl.ds(c * 128 + xv * 32 + z, 8, stride=4), :]
                here = (lane >= base) & (lane < base + 2)
                plus = jnp.where(here, roll_lanes(plane, base - 126), plus)
                minus = jnp.where(here, roll_lanes(plane, base), minus)
        at = CAPY + 8 * xv
        y1[at : at + 8, :] = jnp.where(is_odd, plus, minus)
        y0[at : at + 8, :] = jnp.where(is_odd, minus, plus)
    for fetch in fetches[1:]:
        fetch.wait()


def early_kernel(
    side, tiles_hbm, slots_hbm, weights, rows, vel, back, y1, y0, tiles, slots, held,
    side_list, sems, sem,
):
    for c in range(3):
        back[8 * c : 8 * c + 8, :] = vel[c * 128 : c * 128 + 8, :]

    @pl.when(lax.axis_index("gx") == 0)
    def _():
        sources = (side, tiles_hbm, slots_hbm, rows, vel)
        copies = [weight_copy(weights, 0, held, sem)]
        pack_y(sources, (y1, y0, tiles, slots), side_list, sems, copies)


def late_kernel(
    side, tiles_hbm, slots_hbm, weights, rows, vel, _y1, _y0, _tiles, _slots, _held,
    y1, y0, tiles, slots, held, second, side_list, sems, sem, sem2,
):
    @pl.when(lax.axis_index("gx") != 0)
    def _():
        sources = (side, tiles_hbm, slots_hbm, rows, vel)
        copies = [
            weight_copy(weights, 0, held, sem),
            weight_copy(weights, EARLY, second, sem2),
        ]
        pack_y(sources, (y1, y0, tiles, slots), side_list, sems, copies)


def fill_kernel(weights, held, _second, second, turned, sem):
    copy = weight_copy(weights, EARLY, second, sem)

    @pl.when(lax.axis_index("gx") == 0)
    def _():
        copy.start()

    for n in range(2 * EARLY):
        turned[128 * n : 128 * n + 128, :] = jnp.transpose(held[256 * n : 256 * n + 256, :])

    @pl.when(lax.axis_index("gx") == 0)
    def _():
        copy.wait()


def relay_kernel(upper, lower, _turned, ry1, ry0):
    y_odd = odd("gy")
    for i in range(0, CAPD, 8):
        plus, minus = upper[i : i + 8, :], upper[DIAG1_AT + i : DIAG1_AT + i + 8, :]
        ry1[i : i + 8, :] = jnp.where(y_odd, plus, minus)
        ry0[i : i + 8, :] = jnp.where(y_odd, minus, plus)
    lane = lanes_of((8, 128))
    plus = jnp.zeros((8, 128), F32)
    minus = jnp.zeros((8, 128), F32)
    for c in range(3):
        parts = (upper[VEL_AT + 8 * c : VEL_AT + 8 * c + 8, :], lower[8 * c : 8 * c + 8, :])
        for k, part in enumerate(parts):
            base = (2 * c + k) * 8
            here = (lane >= base) & (lane < base + 2)
            plus = jnp.where(here, roll_lanes(part, base - 126), plus)
            minus = jnp.where(here, roll_lanes(part, base), minus)
    ry1[CAPD:, :] = jnp.where(y_odd, plus, minus)
    ry0[CAPD:, :] = jnp.where(y_odd, minus, plus)


PAIRS = ((0, 0), (1, 1), (2, 2), (0, 1), (0, 2), (1, 2))


def plane_diff(f):
    last = len(f) - 1
    return [
        f[1] - f[0]
        if p == 0
        else f[last] - f[last - 1]
        if p == last
        else (f[p + 1] - f[p - 1]) * 0.5
        for p in range(last + 1)
    ]


def strip_diff(f):
    (f,) = f
    level = lanes_of(f.shape) // 32
    above, below = roll_lanes(f, -32), roll_lanes(f, 32)
    inner = (above - below) * 0.5
    return [jnp.where(level == 0, above - f, jnp.where(level == LZ - 1, f - below, inner))]


def strain(before, here, after, along_z):
    grad = [
        (
            (after[i] - before[i]) * 0.5,
            (roll_lanes(here[i], -1) - roll_lanes(here[i], 1)) * 0.5,
            along_z[i],
        )
        for i in range(3)
    ]
    rate = [grad[i][j] if i == j else 0.5 * (grad[i][j] + grad[j][i]) for i, j in PAIRS]
    own = rate[0] * rate[0] + rate[1] * rate[1] + rate[2] * rate[2]
    cross = rate[3] * rate[3] + rate[4] * rate[4] + rate[5] * rate[5]
    return rate, jnp.sqrt(2.0 * own + 4.0 * cross)


def filtered(before, here, after):
    across = 0.25 * (before + after) + 0.5 * here
    return 0.25 * (roll_lanes(across, 1) + roll_lanes(across, -1)) + 0.5 * across


def stencil(u, q, planes, diff, emit):
    for r in range(0, CX + 8, 8):
        here = [[u[c, p, r + 1 : r + 9, :] for p in range(planes)] for c in range(3)]
        along_z = [diff(here[c]) for c in range(3)]
        for p in range(planes):
            before = [u[c, p, r : r + 8, :] for c in range(3)]
            after = [u[c, p, r + 2 : r + 10, :] for c in range(3)]
            mid = [here[c][p] for c in range(3)]
            rate, size = strain(before, mid, after, [along_z[c][p] for c in range(3)])
            for n, (i, j) in enumerate(PAIRS):
                q[n, p, r : r + 8, :] = size * rate[n]
                q[6 + n, p, r : r + 8, :] = mid[i] * mid[j]
            for c in range(3):
                q[12 + c, p, r : r + 8, :] = filtered(before[c], mid[c], after[c])
    for r in range(0, CX, 8):
        here = [[q[12 + c, p, r + 1 : r + 9, :] for p in range(planes)] for c in range(3)]
        along_z = [diff(here[c]) for c in range(3)]
        for p in range(planes):
            before = [q[12 + c, p, r : r + 8, :] for c in range(3)]
            after = [q[12 + c, p, r + 2 : r + 10, :] for c in range(3)]
            mid = [here[c][p] for c in range(3)]
            rate, size = strain(before, mid, after, [along_z[c][p] for c in range(3)])
            size = 4.0 * size

            def smoothed(n):
                return filtered(
                    q[n, p, r : r + 8, :], q[n, p, r + 1 : r + 9, :], q[n, p, r + 2 : r + 10, :]
                )

            lm, mm = 0.0, 0.0
            for n, (i, j) in enumerate(PAIRS):
                model = 2.0 * (smoothed(n) - size * rate[n])
                leonard = smoothed(6 + n) - mid[i] * mid[j]
                weight = 1.0 if i == j else 2.0
                lm += weight * (leonard * model)
                mm += weight * (model * model)
            emit(p, r, lm, mm)


def candidates(pool, at, value):
    high = value.astype(BF16)
    size = value.shape[0]
    pool[at : at + size, 0:128] = high
    pool[at : at + size, 128:256] = (value - high.astype(F32)).astype(BF16)


def main_kernel(
    vel, upper, lower, y1, y0, rows, tiles, slots, weights,
    lm, mm, strips, partial, diag_picks, third,
    u, q, picks, pool, picked, sem,
):
    fetch = weight_copy(weights, EARLY + SECOND, third, sem)

    @pl.when(lax.axis_index("gx") >= 0)
    def _():
        fetch.start()

    y_odd = odd("gy")
    lane = lanes_of((8, 128))
    for c in range(3):
        for z in range(LZ):
            u[c, z, 0:2, :] = upper[pl.ds(VEL_AT + 8 * c + z, 2, stride=4), :]
            u[c, z, 2 : CX + 2, :] = vel[pl.ds(c * 128 + z, CX, stride=4), :]
            u[c, z, CX + 2 : CX + 4, :] = lower[pl.ds(8 * c + z, 2, stride=4), :]
    for c in range(3):
        for r in range(0, CX + 8, 8):
            strip = jnp.zeros((8, 128), F32)
            for z in range(LZ):
                base = 32 * z
                plane = u[c, z, r : r + 8, :]
                left = (lane >= base + 2) & (lane < base + 6)
                right = (lane >= base + 16) & (lane < base + 20)
                strip = jnp.where(left, roll_lanes(plane, base + 2), strip)
                strip = jnp.where(right, roll_lanes(plane, base + 16 - 124), strip)
            strips[c, r : r + 8, :] = strip
        for r in range(0, CX, 8):
            at = CAPY + r
            low = jnp.where(y_odd, y0[at : at + 8, :], y1[at : at + 8, :])
            high = jnp.where(y_odd, y1[at : at + 8, :], y0[at : at + 8, :])
            strip = strips[c, r + 2 : r + 10, :]
            strip = jnp.where(lane % 32 < 2, roll_lanes(low, -8 * c), strip)
            here = (lane % 32 >= 20) & (lane % 32 < 22)
            strip = jnp.where(here, roll_lanes(high, 20 - 8 * c), strip)
            strips[c, r + 2 : r + 10, :] = strip

    def emit(z, r, lm_part, mm_part):
        for k in range(2):
            lm[pl.ds(8 * r + 2 * z + k, 8, stride=8), :] = lm_part
            mm[pl.ds(8 * r + 2 * z + k, 8, stride=8), :] = mm_part

    stencil(u, q, LZ, plane_diff, emit)

    tile = tiles[...]
    starts = (0, UP_POOL, LOW_POOL, HIGH_POOL, DIAG_LOW_POOL, DIAG_HIGH_POOL)
    index = slots[...]
    for n, start in enumerate(starts):
        index = index + jnp.where(tile == n, start, 0)
    index = index.astype(F32)
    column = lanes_of((128, 128)).astype(F32)
    hits = []
    for k in range(2):
        for half in range(2):
            line = index[k : k + 1, half * 128 : half * 128 + 128]
            wanted = jnp.transpose(jnp.broadcast_to(line, (128, 128)))
            at = k * NBD + half * 128
            for part in range(POOL // 128):
                hit = jnp.where(wanted == column + 128.0 * part, 1.0, 0.0)
                picks[at : at + 128, part * 128 : part * 128 + 128] = hit.astype(BF16)
            hit = (wanted - (POOL - 64.0 * k)) == column
            mine = (column >= 64.0) if k else (column < 64.0)
            hits.append(jnp.where(hit & mine, 1.0, 0.0))
    for half in range(2):
        diag_picks[half * 128 : half * 128 + 128, :] = (hits[half] + hits[2 + half]).astype(BF16)
    candidates(pool, 0, rows[...])
    candidates(pool, UP_POOL, upper[UP_AT:, :])
    candidates(pool, LOW_POOL, jnp.where(y_odd, y0[:CAPY, :], y1[:CAPY, :]))
    candidates(pool, HIGH_POOL, jnp.where(y_odd, y1[:CAPY, :], y0[:CAPY, :]))
    picked[...] = jnp.dot(picks[...], pool[...], preferred_element_type=F32)
    front = lane < 64
    for r in range(0, NBD, 8):
        for n in range(2):
            first = picked[r : r + 8, 128 * n : 128 * n + 128]
            second = picked[NBD + r : NBD + r + 8, 128 * n : 128 * n + 128]
            partial[r : r + 8, 128 * n : 128 * n + 128] = jnp.where(
                front, first, roll_lanes(second, 64)
            )
            partial[r : r + 8, 256 + 128 * n : 384 + 128 * n] = jnp.where(
                front, roll_lanes(first, 64), second
            )
    fetch.wait()


def final_kernel(
    lm_in, mm_in, strips, ry1, ry0, partial, picks, turned, second, third, out,
    u, q, lm, mm, pool, picked, lefts, departs,
):
    y_odd = odd("gy")
    lane = lanes_of((8, 128))
    lm[...] = lm_in[...]
    mm[...] = mm_in[...]

    diag = jnp.concatenate(
        [
            jnp.where(y_odd, ry0[:CAPD, :], ry1[:CAPD, :]),
            jnp.where(y_odd, ry1[:CAPD, :], ry0[:CAPD, :]),
        ],
        axis=0,
    )
    high = diag.astype(BF16).astype(F32)
    front = lanes_of((2 * CAPD, 128)) < 64
    for n, term in enumerate((high, diag - high)):
        swapped = roll_lanes(term, 64)
        for at, value in (
            (128 * n, (jnp.where(front, term, 0.0), jnp.where(front, 0.0, swapped))),
            (256 + 128 * n, (jnp.where(front, swapped, 0.0), jnp.where(front, 0.0, term))),
        ):
            pool[: 2 * CAPD, at : at + 128] = value[0].astype(BF16)
            pool[2 * CAPD :, at : at + 128] = value[1].astype(BF16)
    picked[...] = partial[...] + jnp.dot(picks[...], pool[...], preferred_element_type=F32)

    low = jnp.where(y_odd, ry0[CAPD:, :], ry1[CAPD:, :])
    high = jnp.where(y_odd, ry1[CAPD:, :], ry0[CAPD:, :])
    u[...] = strips[...].reshape(u.shape)
    for c in range(3):
        for k, at in enumerate((0, CX + 2)):
            base = (2 * c + k) * 8
            for x in range(2):
                row = u[c, 0, at + x : at + x + 1, :]
                one = lanes_of((1, 128))
                for z in range(LZ):
                    line = low[4 * x + z : 4 * x + z + 1, :]
                    here = (one >= 32 * z) & (one < 32 * z + 2)
                    row = jnp.where(here, roll_lanes(line, 32 * z - base), row)
                    line = high[4 * x + z : 4 * x + z + 1, :]
                    here = (one >= 32 * z + 20) & (one < 32 * z + 22)
                    row = jnp.where(here, roll_lanes(line, 32 * z + 20 - base), row)
                u[c, 0, at + x : at + x + 1, :] = row

    def emit(_, r, lm_part, mm_part):
        for into, part in ((lm, lm_part), (mm, mm_part)):
            for z in range(LZ):
                left = roll_lanes(part, -(32 * z + 2))
                right = roll_lanes(part, 126 - (32 * z + 18))
                for k in range(2):
                    at = pl.ds(8 * r + 2 * z + k, 8, stride=8)
                    value = jnp.where(lane < 2, left, jnp.where(lane >= 126, right, into[at, :]))
                    into[at, :] = value

    stencil(u, q, 1, strip_diff, emit)

    row_of = lax.broadcasted_iota(jnp.int32, (8, 128), 0)
    top = lax.broadcasted_iota(jnp.int32, (16, 128), 0) % 8 < 4
    for x in range(CX):
        for n in range(2):
            left = jnp.concatenate(
                [
                    picked[8 * x : 8 * x + 8, 128 * n + at : 128 * n + at + 128]
                    for at in (0, 256)
                ],
                axis=0,
            )
            at = 32 * x + 16 * n
            lefts[at : at + 16, :128] = jnp.where(top, left, 0.0).astype(BF16)
            lefts[at : at + 16, 128:] = jnp.where(top, 0.0, left).astype(BF16)
    for x in range(CX):
        if x < EARLY:
            right, over = turned[256 * x : 256 * x + 256, :], 0
        else:
            late = x >= EARLY + SECOND
            held, at = (third, x - EARLY - SECOND) if late else (second, x - EARLY)
            at = GROUP * at
            right = jnp.concatenate([held[at : at + 256, :], held[at + 256 : at + 512, :]], axis=1)
            over = 1
        product = lax.dot_general(
            lefts[32 * x : 32 * x + 32, :],
            right,
            (((1,), (over,)), ((), ())),
            preferred_element_type=F32,
        )
        product = product[:16] + product[16:]
        for n in range(2):
            part = product[8 * n : 8 * n + 8, :]
            departs[n, 8 * x : 8 * x + 8, :] = jnp.where(
                row_of % 4 < 2, part[:, :128], part[:, 128:]
            )

    front = lane < 64
    even = row_of % 2 == 0
    for x in range(CX):
        lm_depart = departs[0, 8 * x : 8 * x + 8, :]
        mm_depart = departs[1, 8 * x : 8 * x + 8, :]
        lm_block, mm_block = lm[8 * x : 8 * x + 8, :], mm[8 * x : 8 * x + 8, :]
        ratio = (TIME_STEP / 1.5) * jnp.exp(0.125 * jnp.log(lm_depart * mm_depart))
        weight = ratio / (1.0 + ratio)
        lm_next = jnp.maximum(weight * lm_block + (1.0 - weight) * lm_depart, 0.0)
        mm_next = weight * mm_block + (1.0 - weight) * mm_depart
        lm_next = jnp.where(even, lm_next, roll_lanes(lm_next, 64))
        mm_next = jnp.where(even, roll_lanes(mm_next, 64), mm_next)
        out[8 * x : 8 * x + 8, :] = jnp.where(front, lm_next, mm_next)


def vmem(count=1):
    return [pl.BlockSpec(memory_space=pltpu.VMEM)] * count


def hbm(count=1):
    return [pl.BlockSpec(memory_space=pltpu.HBM)] * count


def array(*shape, dtype=F32):
    return jax.ShapeDtypeStruct(shape, dtype)


def call(kernel, ins, outs, scratch=(), cost=1000, aliases=()):
    return pl.pallas_call(
        kernel,
        in_specs=ins,
        out_specs=tuple(vmem(len(outs))) if isinstance(outs, tuple) else vmem()[0],
        out_shape=outs,
        scratch_shapes=list(scratch),
        input_output_aliases=dict(aliases),
        compiler_params=pltpu.CompilerParams(vmem_limit_bytes=32 * 1024 * 1024),
        cost_estimate=pl.CostEstimate(flops=cost, bytes_accessed=cost, transcendentals=0),
    )


def swap(block, axis, start):
    count = lax.axis_size(axis)
    ahead = [(i, (i + 1) % count) for i in range(start, count, 2)]
    return lax.ppermute(block, axis, ahead + [(j, i) for i, j in ahead])


def shift(block, axis, distance):
    count = lax.axis_size(axis)
    return lax.ppermute(block, axis, [(i, (i + distance) % count) for i in range(count)])


def on_device(
    velocity, pair_blocks, send_up, send_side, send_diag, depart_tile, depart_slot, interp_weights
):
    def stay(x):
        return pltpu.with_memory_space_constraint(x, pltpu.HBM)

    vel = stay(velocity.reshape(3 * CX * LZ, 128))
    rows = stay(pair_blocks[0, 0])
    weights = stay(interp_weights.reshape(NBD * 64, 128))
    up, side, diag = stay(send_up[0, 0]), stay(send_side[0, 0]), stay(send_diag[0, 0])
    tiles, slots = stay(depart_tile[0, 0]), stay(depart_slot[0, 0])

    ahead, held_rows, held_vel = call(
        pack_x_kernel,
        hbm(4),
        (array(X_ROWS, 128), array(*rows.shape), array(*vel.shape)),
        [
            pltpu.SMEM((CAPX,), jnp.int32),
            pltpu.SMEM((2, CAPD), jnp.int32),
            pltpu.SemaphoreType.DMA((4,)),
        ],
    )(up, diag, rows, vel)
    upper = shift(ahead, "gx", 1)
    def held(count):
        return array(count * GROUP, 128, dtype=BF16)

    packed = (
        array(Y_ROWS, 128),
        array(Y_ROWS, 128),
        array(*tiles.shape, dtype=jnp.int32),
        array(*slots.shape, dtype=jnp.int32),
        held(EARLY),
    )
    scratch = [pltpu.SMEM((2, CAPY), jnp.int32), pltpu.SemaphoreType.DMA((3,))]
    sources = (side, tiles, slots, weights, held_rows, held_vel)
    back, *early = call(
        early_kernel,
        hbm(4) + vmem(2),
        (array(BACK_ROWS, 128),) + packed,
        scratch + [pltpu.SemaphoreType.DMA],
    )(*sources)
    lower = shift(back, "gx", -1)
    y1, y0, held_tiles, held_slots, first, second = call(
        late_kernel,
        hbm(4) + vmem(7),
        packed + (held(SECOND),),
        scratch + [pltpu.SemaphoreType.DMA] * 2,
        aliases=((6 + n, n) for n in range(5)),
    )(*sources, *early)
    y1 = swap(y1, "gy", 1)
    y0 = swap(y0, "gy", 0)
    second, turned = call(
        fill_kernel,
        hbm() + vmem(2),
        (held(SECOND), array(EARLY * 256, 256, dtype=BF16)),
        [pltpu.SemaphoreType.DMA],
        aliases=((2, 0),),
    )(weights, first, second)
    ry1, ry0 = call(relay_kernel, vmem(3), (array(R_ROWS, 128),) * 2, cost=300000000)(upper, lower, turned)
    ry1 = swap(ry1, "gy", 1)
    ry0 = swap(ry0, "gy", 0)
    lm, mm, strips, partial, picks, third = call(
        main_kernel,
        vmem(8) + hbm(),
        (
            array(NBD, 128),
            array(NBD, 128),
            array(3, EXT, 128),
            array(NBD, 512),
            array(NBD, POOL_DIAG, dtype=BF16),
            held(NBD // 8 - EARLY - SECOND),
        ),
        [
            pltpu.VMEM((3, LZ, EXT, 128), F32),
            pltpu.VMEM((15, LZ, EXT, 128), F32),
            pltpu.VMEM((2 * NBD, POOL), BF16),
            pltpu.VMEM((POOL, 256), BF16),
            pltpu.VMEM((2 * NBD, 256), F32),
            pltpu.SemaphoreType.DMA,
        ],
        cost=5000000,
    )(held_vel, upper, lower, y1, y0, held_rows, held_tiles, held_slots, weights)
    result = call(
        final_kernel,
        vmem(10),
        array(NBD, 128),
        [
            pltpu.VMEM((3, 1, EXT, 128), F32),
            pltpu.VMEM((15, 1, EXT, 128), F32),
            pltpu.VMEM((NBD, 128), F32),
            pltpu.VMEM((NBD, 128), F32),
            pltpu.VMEM((POOL_DIAG, 512), BF16),
            pltpu.VMEM((NBD, 512), F32),
            pltpu.VMEM((4 * NBD, 256), BF16),
            pltpu.VMEM((2, NBD, 128), F32),
        ],
    )(lm, mm, strips, ry1, ry0, partial, picks, turned, second, third)
    return result[None, None]


def solution(mesh):
    return jax.shard_map(
        on_device,
        mesh=mesh,
        in_specs=(
            P(None, "gx", None, "gy"),
            P("gx", "gy", None, None),
            P("gx", "gy", None),
            P("gx", "gy", None, None),
            P("gx", "gy", None, None),
            P("gx", "gy", None, None),
            P("gx", "gy", None, None),
            P("gx", "gy", None, None, None),
        ),
        out_specs=P("gx", "gy", None, None),
        check_vma=False,
    )
```

```python
import functools

import jax
import jax.numpy as jnp
from jax import lax
from jax.experimental import pallas as pl
from jax.experimental.pallas import tpu as pltpu
from jax.sharding import PartitionSpec as P

CX = 32
LZ = 4
NBD = 256
CAPX = 128
CAPY = 64
CAPD = 32

TIME_STEP = 0.5

VEL_AT = CAPD
DIAG1_AT = CAPD + 24
UP_AT = 2 * CAPD + 24
X_ROWS = UP_AT + CAPX
BACK_ROWS = 24
Y_ROWS = CAPY + CX
R_ROWS = CAPD + 8

POOL = NBD + CAPX + 2 * CAPY
POOL_DIAG = 128
UP_POOL = NBD
LOW_POOL = NBD + CAPX
HIGH_POOL = LOW_POOL + CAPY
DIAG_LOW_POOL = HIGH_POOL + CAPY
DIAG_HIGH_POOL = DIAG_LOW_POOL + CAPD

EXT = 48
GROUP = 8 * 64
EARLY = 12
SECOND = 6
F32 = jnp.float32
BF16 = jnp.bfloat16


def lanes_of(shape):
    return lax.broadcasted_iota(jnp.int32, shape, 1)


def roll_lanes(x, shift):
    shift = shift % 128
    return x if shift == 0 else pltpu.roll(x, shift, 1)


def odd(axis):
    return lax.rem(lax.axis_index(axis), 2) == 1


def pack_x_kernel(
    up_hbm, diag_hbm, rows_hbm, vel_hbm, ahead, rows, vel, up_list, diag_list, sems
):
    fetches = [
        pltpu.make_async_copy(source, target, sems.at[n])
        for n, (source, target) in enumerate(
            ((up_hbm, up_list), (diag_hbm, diag_list), (rows_hbm, rows), (vel_hbm, vel))
        )
    ]
    for fetch in fetches:
        fetch.start()
    for fetch in fetches[:3]:
        fetch.wait()
    for i in range(CAPD):
        ahead[i : i + 1, :] = rows[pl.ds(diag_list[0, i], 1), :]
        ahead[DIAG1_AT + i : DIAG1_AT + i + 1, :] = rows[pl.ds(diag_list[1, i], 1), :]
    for i in range(CAPX):
        ahead[UP_AT + i : UP_AT + i + 1, :] = rows[pl.ds(up_list[i], 1), :]
    fetches[3].wait()
    for c in range(3):
        ahead[VEL_AT + 8 * c : VEL_AT + 8 * c + 8, :] = vel[c * 128 + 120 : c * 128 + 128, :]


def weight_copy(weights, start, held, sem):
    return pltpu.make_async_copy(weights.at[pl.ds(start * GROUP, held.shape[0]), :], held, sem)


def pack_y(sources, outs, side_list, sems, weight_copies):
    side_hbm, tiles_hbm, slots_hbm, rows, vel = sources
    y1, y0, tiles, slots = outs
    is_odd = odd("gy")
    first = jnp.where(is_odd, 0, 1)
    fetches = [
        pltpu.make_async_copy(source, target, sems.at[n])
        for n, (source, target) in enumerate(
            ((side_hbm, side_list), (tiles_hbm, tiles), (slots_hbm, slots))
        )
    ]
    fetches += weight_copies
    for fetch in fetches:
        fetch.start()
    fetches[0].wait()
    for i in range(CAPY):
        y1[i : i + 1, :] = rows[pl.ds(side_list[first, i], 1), :]
        y0[i : i + 1, :] = rows[pl.ds(side_list[1 - first, i], 1), :]
    lane = lanes_of((8, 128))
    for xv in range(4):
        plus = jnp.zeros((8, 128), F32)
        minus = jnp.zeros((8, 128), F32)
        for z in range(LZ):
            for c in range(3):
                base = z * 32 + c * 8
                plane = vel[pl.ds(c * 128 + xv * 32 + z, 8, stride=4), :]
                here = (lane >= base) & (lane < base + 2)
                plus = jnp.where(here, roll_lanes(plane, base - 126), plus)
                minus = jnp.where(here, roll_lanes(plane, base), minus)
        at = CAPY + 8 * xv
        y1[at : at + 8, :] = jnp.where(is_odd, plus, minus)
        y0[at : at + 8, :] = jnp.where(is_odd, minus, plus)
    for fetch in fetches[1:]:
        fetch.wait()


def early_kernel(
    side, tiles_hbm, slots_hbm, weights, rows, vel, back, y1, y0, tiles, slots, held,
    side_list, sems, sem,
):
    for c in range(3):
        back[8 * c : 8 * c + 8, :] = vel[c * 128 : c * 128 + 8, :]

    @pl.when(lax.axis_index("gx") == 0)
    def _():
        sources = (side, tiles_hbm, slots_hbm, rows, vel)
        copies = [weight_copy(weights, 0, held, sem)]
        pack_y(sources, (y1, y0, tiles, slots), side_list, sems, copies)


def late_kernel(
    side, tiles_hbm, slots_hbm, weights, rows, vel, y1_early, y0_early, tiles_early, slots_early,
    y1, y0, tiles, slots, held, second, side_list, sems, sem, sem2,
):
    @pl.when(lax.axis_index("gx") == 0)
    def _():
        y1[...] = y1_early[...]
        y0[...] = y0_early[...]
        tiles[...] = tiles_early[...]
        slots[...] = slots_early[...]

    @pl.when(lax.axis_index("gx") != 0)
    def _():
        sources = (side, tiles_hbm, slots_hbm, rows, vel)
        copies = [
            weight_copy(weights, 0, held, sem),
            weight_copy(weights, EARLY, second, sem2),
        ]
        pack_y(sources, (y1, y0, tiles, slots), side_list, sems, copies)


def turn(held, turned):
    for n in range(2 * EARLY):
        turned[128 * n : 128 * n + 128, :] = jnp.transpose(held[256 * n : 256 * n + 256, :])


def fill_kernel(weights, held_early, held_late, second_late, second, turned, sem):
    copy = weight_copy(weights, EARLY, second, sem)

    @pl.when(lax.axis_index("gx") == 0)
    def _():
        copy.start()

        @after_start
        def _():
            turn(held_early, turned)

        copy.wait()

    @pl.when(lax.axis_index("gx") != 0)
    def _():
        second[...] = second_late[...]
        turn(held_late, turned)


def relay_kernel(upper, lower, _turned, ry1, ry0):
    y_odd = odd("gy")
    for i in range(0, CAPD, 8):
        plus, minus = upper[i : i + 8, :], upper[DIAG1_AT + i : DIAG1_AT + i + 8, :]
        ry1[i : i + 8, :] = jnp.where(y_odd, plus, minus)
        ry0[i : i + 8, :] = jnp.where(y_odd, minus, plus)
    lane = lanes_of((8, 128))
    plus = jnp.zeros((8, 128), F32)
    minus = jnp.zeros((8, 128), F32)
    for c in range(3):
        parts = (upper[VEL_AT + 8 * c : VEL_AT + 8 * c + 8, :], lower[8 * c : 8 * c + 8, :])
        for k, part in enumerate(parts):
            base = (2 * c + k) * 8
            here = (lane >= base) & (lane < base + 2)
            plus = jnp.where(here, roll_lanes(part, base - 126), plus)
            minus = jnp.where(here, roll_lanes(part, base), minus)
    ry1[CAPD:, :] = jnp.where(y_odd, plus, minus)
    ry0[CAPD:, :] = jnp.where(y_odd, minus, plus)


PAIRS = ((0, 0), (1, 1), (2, 2), (0, 1), (0, 2), (1, 2))


def plane_diff(f):
    last = len(f) - 1
    return [
        f[1] - f[0]
        if p == 0
        else f[last] - f[last - 1]
        if p == last
        else (f[p + 1] - f[p - 1]) * 0.5
        for p in range(last + 1)
    ]


def strip_diff(f):
    (f,) = f
    level = lanes_of(f.shape) // 32
    above, below = roll_lanes(f, -32), roll_lanes(f, 32)
    inner = (above - below) * 0.5
    return [jnp.where(level == 0, above - f, jnp.where(level == LZ - 1, f - below, inner))]


def strain(before, here, after, along_z):
    grad = [
        (
            (after[i] - before[i]) * 0.5,
            (roll_lanes(here[i], -1) - roll_lanes(here[i], 1)) * 0.5,
            along_z[i],
        )
        for i in range(3)
    ]
    rate = [grad[i][j] if i == j else 0.5 * (grad[i][j] + grad[j][i]) for i, j in PAIRS]
    own = rate[0] * rate[0] + rate[1] * rate[1] + rate[2] * rate[2]
    cross = rate[3] * rate[3] + rate[4] * rate[4] + rate[5] * rate[5]
    return rate, jnp.sqrt(2.0 * own + 4.0 * cross)


def filtered(before, here, after):
    across = 0.25 * (before + after) + 0.5 * here
    return 0.25 * (roll_lanes(across, 1) + roll_lanes(across, -1)) + 0.5 * across


def stencil(u, q, planes, diff, emit):
    for r in range(0, CX + 8, 8):
        here = [[u[c, p, r + 1 : r + 9, :] for p in range(planes)] for c in range(3)]
        along_z = [diff(here[c]) for c in range(3)]
        for p in range(planes):
            before = [u[c, p, r : r + 8, :] for c in range(3)]
            after = [u[c, p, r + 2 : r + 10, :] for c in range(3)]
            mid = [here[c][p] for c in range(3)]
            rate, size = strain(before, mid, after, [along_z[c][p] for c in range(3)])
            for n, (i, j) in enumerate(PAIRS):
                q[n, p, r : r + 8, :] = size * rate[n]
                q[6 + n, p, r : r + 8, :] = mid[i] * mid[j]
            for c in range(3):
                q[12 + c, p, r : r + 8, :] = filtered(before[c], mid[c], after[c])
    for r in range(0, CX, 8):
        here = [[q[12 + c, p, r + 1 : r + 9, :] for p in range(planes)] for c in range(3)]
        along_z = [diff(here[c]) for c in range(3)]
        for p in range(planes):
            before = [q[12 + c, p, r : r + 8, :] for c in range(3)]
            after = [q[12 + c, p, r + 2 : r + 10, :] for c in range(3)]
            mid = [here[c][p] for c in range(3)]
            rate, size = strain(before, mid, after, [along_z[c][p] for c in range(3)])
            size = 4.0 * size

            def smoothed(n):
                return filtered(
                    q[n, p, r : r + 8, :], q[n, p, r + 1 : r + 9, :], q[n, p, r + 2 : r + 10, :]
                )

            lm, mm = 0.0, 0.0
            for n, (i, j) in enumerate(PAIRS):
                model = 2.0 * (smoothed(n) - size * rate[n])
                leonard = smoothed(6 + n) - mid[i] * mid[j]
                weight = 1.0 if i == j else 2.0
                lm += weight * (leonard * model)
                mm += weight * (model * model)
            emit(p, r, lm, mm)


def after_start(body):
    pl.loop(0, jnp.where(lax.axis_index("gx") >= 0, 1, 0))(lambda _: body())


def candidates(pool, at, value):
    high = value.astype(BF16)
    size = value.shape[0]
    pool[at : at + size, 0:128] = high
    pool[at : at + size, 128:256] = (value - high.astype(F32)).astype(BF16)


def main_kernel(
    vel, upper, lower, y1, y0, rows, tiles, slots, weights,
    lm, mm, strips, partial, diag_picks, third,
    u, q, picks, pool, picked, sem,
):
    fetch = weight_copy(weights, EARLY + SECOND, third, sem)

    fetch.start()

    @after_start
    def _():
        y_odd = odd("gy")
        lane = lanes_of((8, 128))
        for c in range(3):
            for z in range(LZ):
                u[c, z, 0:2, :] = upper[pl.ds(VEL_AT + 8 * c + z, 2, stride=4), :]
                u[c, z, 2 : CX + 2, :] = vel[pl.ds(c * 128 + z, CX, stride=4), :]
                u[c, z, CX + 2 : CX + 4, :] = lower[pl.ds(8 * c + z, 2, stride=4), :]
        for c in range(3):
            for r in range(0, CX + 8, 8):
                strip = jnp.zeros((8, 128), F32)
                for z in range(LZ):
                    base = 32 * z
                    plane = u[c, z, r : r + 8, :]
                    left = (lane >= base + 2) & (lane < base + 6)
                    right = (lane >= base + 16) & (lane < base + 20)
                    strip = jnp.where(left, roll_lanes(plane, base + 2), strip)
                    strip = jnp.where(right, roll_lanes(plane, base + 16 - 124), strip)
                strips[c, r : r + 8, :] = strip
            for r in range(0, CX, 8):
                at = CAPY + r
                low = jnp.where(y_odd, y0[at : at + 8, :], y1[at : at + 8, :])
                high = jnp.where(y_odd, y1[at : at + 8, :], y0[at : at + 8, :])
                strip = strips[c, r + 2 : r + 10, :]
                strip = jnp.where(lane % 32 < 2, roll_lanes(low, -8 * c), strip)
                here = (lane % 32 >= 20) & (lane % 32 < 22)
                strip = jnp.where(here, roll_lanes(high, 20 - 8 * c), strip)
                strips[c, r + 2 : r + 10, :] = strip

        def emit(z, r, lm_part, mm_part):
            for k in range(2):
                lm[pl.ds(8 * r + 2 * z + k, 8, stride=8), :] = lm_part
                mm[pl.ds(8 * r + 2 * z + k, 8, stride=8), :] = mm_part

        stencil(u, q, LZ, plane_diff, emit)

        tile = tiles[...]
        starts = (0, UP_POOL, LOW_POOL, HIGH_POOL, DIAG_LOW_POOL, DIAG_HIGH_POOL)
        index = slots[...]
        for n, start in enumerate(starts):
            index = index + jnp.where(tile == n, start, 0)
        index = index.astype(F32)
        column = lanes_of((128, 128)).astype(F32)
        hits = []
        for k in range(2):
            for half in range(2):
                line = index[k : k + 1, half * 128 : half * 128 + 128]
                wanted = jnp.transpose(jnp.broadcast_to(line, (128, 128)))
                at = k * NBD + half * 128
                for part in range(POOL // 128):
                    hit = jnp.where(wanted == column + 128.0 * part, 1.0, 0.0)
                    picks[at : at + 128, part * 128 : part * 128 + 128] = hit.astype(BF16)
                hit = (wanted - (POOL - 64.0 * k)) == column
                mine = (column >= 64.0) if k else (column < 64.0)
                hits.append(jnp.where(hit & mine, 1.0, 0.0))
        for half in range(2):
            diag_picks[half * 128 : half * 128 + 128, :] = (hits[half] + hits[2 + half]).astype(BF16)
        candidates(pool, 0, rows[...])
        candidates(pool, UP_POOL, upper[UP_AT:, :])
        candidates(pool, LOW_POOL, jnp.where(y_odd, y0[:CAPY, :], y1[:CAPY, :]))
        candidates(pool, HIGH_POOL, jnp.where(y_odd, y1[:CAPY, :], y0[:CAPY, :]))
        picked[...] = jnp.dot(picks[...], pool[...], preferred_element_type=F32)
        front = lane < 64
        for r in range(0, NBD, 8):
            for n in range(2):
                first = picked[r : r + 8, 128 * n : 128 * n + 128]
                second = picked[NBD + r : NBD + r + 8, 128 * n : 128 * n + 128]
                partial[r : r + 8, 128 * n : 128 * n + 128] = jnp.where(
                    front, first, roll_lanes(second, 64)
                )
                partial[r : r + 8, 256 + 128 * n : 384 + 128 * n] = jnp.where(
                    front, roll_lanes(first, 64), second
                )

    fetch.wait()


def final_kernel(
    lm_in, mm_in, strips, ry1, ry0, partial, picks, turned, second, third, out,
    u, q, lm, mm, pool, picked, lefts, departs,
):
    y_odd = odd("gy")
    lane = lanes_of((8, 128))
    lm[...] = lm_in[...]
    mm[...] = mm_in[...]

    diag = jnp.concatenate(
        [
            jnp.where(y_odd, ry0[:CAPD, :], ry1[:CAPD, :]),
            jnp.where(y_odd, ry1[:CAPD, :], ry0[:CAPD, :]),
        ],
        axis=0,
    )
    high = diag.astype(BF16).astype(F32)
    front = lanes_of((2 * CAPD, 128)) < 64
    for n, term in enumerate((high, diag - high)):
        swapped = roll_lanes(term, 64)
        for at, value in (
            (128 * n, (jnp.where(front, term, 0.0), jnp.where(front, 0.0, swapped))),
            (256 + 128 * n, (jnp.where(front, swapped, 0.0), jnp.where(front, 0.0, term))),
        ):
            pool[: 2 * CAPD, at : at + 128] = value[0].astype(BF16)
            pool[2 * CAPD :, at : at + 128] = value[1].astype(BF16)
    picked[...] = partial[...] + jnp.dot(picks[...], pool[...], preferred_element_type=F32)

    low = jnp.where(y_odd, ry0[CAPD:, :], ry1[CAPD:, :])
    high = jnp.where(y_odd, ry1[CAPD:, :], ry0[CAPD:, :])
    u[...] = strips[...].reshape(u.shape)
    for c in range(3):
        for k, at in enumerate((0, CX + 2)):
            base = (2 * c + k) * 8
            for x in range(2):
                row = u[c, 0, at + x : at + x + 1, :]
                one = lanes_of((1, 128))
                for z in range(LZ):
                    line = low[4 * x + z : 4 * x + z + 1, :]
                    here = (one >= 32 * z) & (one < 32 * z + 2)
                    row = jnp.where(here, roll_lanes(line, 32 * z - base), row)
                    line = high[4 * x + z : 4 * x + z + 1, :]
                    here = (one >= 32 * z + 20) & (one < 32 * z + 22)
                    row = jnp.where(here, roll_lanes(line, 32 * z + 20 - base), row)
                u[c, 0, at + x : at + x + 1, :] = row

    def emit(_, r, lm_part, mm_part):
        for into, part in ((lm, lm_part), (mm, mm_part)):
            for z in range(LZ):
                left = roll_lanes(part, -(32 * z + 2))
                right = roll_lanes(part, 126 - (32 * z + 18))
                for k in range(2):
                    at = pl.ds(8 * r + 2 * z + k, 8, stride=8)
                    value = jnp.where(lane < 2, left, jnp.where(lane >= 126, right, into[at, :]))
                    into[at, :] = value

    stencil(u, q, 1, strip_diff, emit)

    row_of = lax.broadcasted_iota(jnp.int32, (8, 128), 0)
    top = lax.broadcasted_iota(jnp.int32, (16, 128), 0) % 8 < 4
    for x in range(CX):
        for n in range(2):
            left = jnp.concatenate(
                [
                    picked[8 * x : 8 * x + 8, 128 * n + at : 128 * n + at + 128]
                    for at in (0, 256)
                ],
                axis=0,
            )
            at = 32 * x + 16 * n
            lefts[at : at + 16, :128] = jnp.where(top, left, 0.0).astype(BF16)
            lefts[at : at + 16, 128:] = jnp.where(top, 0.0, left).astype(BF16)
    for x in range(CX):
        if x < EARLY:
            right, over = turned[256 * x : 256 * x + 256, :], 0
        else:
            late = x >= EARLY + SECOND
            held, at = (third, x - EARLY - SECOND) if late else (second, x - EARLY)
            at = GROUP * at
            right = jnp.concatenate([held[at : at + 256, :], held[at + 256 : at + 512, :]], axis=1)
            over = 1
        product = lax.dot_general(
            lefts[32 * x : 32 * x + 32, :],
            right,
            (((1,), (over,)), ((), ())),
            preferred_element_type=F32,
        )
        product = product[:16] + product[16:]
        for n in range(2):
            part = product[8 * n : 8 * n + 8, :]
            departs[n, 8 * x : 8 * x + 8, :] = jnp.where(
                row_of % 4 < 2, part[:, :128], part[:, 128:]
            )

    front = lane < 64
    even = row_of % 2 == 0
    for x in range(CX):
        lm_depart = departs[0, 8 * x : 8 * x + 8, :]
        mm_depart = departs[1, 8 * x : 8 * x + 8, :]
        lm_block, mm_block = lm[8 * x : 8 * x + 8, :], mm[8 * x : 8 * x + 8, :]
        ratio = (TIME_STEP / 1.5) * jnp.exp(0.125 * jnp.log(lm_depart * mm_depart))
        weight = ratio / (1.0 + ratio)
        lm_next = jnp.maximum(weight * lm_block + (1.0 - weight) * lm_depart, 0.0)
        mm_next = weight * mm_block + (1.0 - weight) * mm_depart
        lm_next = jnp.where(even, lm_next, roll_lanes(lm_next, 64))
        mm_next = jnp.where(even, roll_lanes(mm_next, 64), mm_next)
        out[8 * x : 8 * x + 8, :] = jnp.where(front, lm_next, mm_next)


def vmem(count=1):
    return [pl.BlockSpec(memory_space=pltpu.VMEM)] * count


def hbm(count=1):
    return [pl.BlockSpec(memory_space=pltpu.HBM)] * count


def array(*shape, dtype=F32):
    return jax.ShapeDtypeStruct(shape, dtype)


def call(kernel, ins, outs, scratch=(), cost=1000):
    return pl.pallas_call(
        kernel,
        in_specs=ins,
        out_specs=tuple(vmem(len(outs))) if isinstance(outs, tuple) else vmem()[0],
        out_shape=outs,
        scratch_shapes=list(scratch),
        compiler_params=pltpu.CompilerParams(vmem_limit_bytes=32 * 1024 * 1024),
        cost_estimate=pl.CostEstimate(flops=cost, bytes_accessed=cost, transcendentals=0),
    )


def swap(block, axis, start):
    count = lax.axis_size(axis)
    ahead = [(i, (i + 1) % count) for i in range(start, count, 2)]
    return lax.ppermute(block, axis, ahead + [(j, i) for i, j in ahead])


def shift(block, axis, distance):
    count = lax.axis_size(axis)
    return lax.ppermute(block, axis, [(i, (i + distance) % count) for i in range(count)])


def on_device(
    velocity, pair_blocks, send_up, send_side, send_diag, depart_tile, depart_slot, interp_weights
):
    def stay(x):
        return pltpu.with_memory_space_constraint(x, pltpu.HBM)

    vel = stay(velocity.reshape(3 * CX * LZ, 128))
    rows = stay(pair_blocks[0, 0])
    weights = stay(interp_weights.reshape(NBD * 64, 128))
    up, side, diag = stay(send_up[0, 0]), stay(send_side[0, 0]), stay(send_diag[0, 0])
    tiles, slots = stay(depart_tile[0, 0]), stay(depart_slot[0, 0])

    ahead, held_rows, held_vel = call(
        pack_x_kernel,
        hbm(4),
        (array(X_ROWS, 128), array(*rows.shape), array(*vel.shape)),
        [
            pltpu.SMEM((CAPX,), jnp.int32),
            pltpu.SMEM((2, CAPD), jnp.int32),
            pltpu.SemaphoreType.DMA((4,)),
        ],
    )(up, diag, rows, vel)
    upper = shift(ahead, "gx", 1)

    def held(count):
        return array(count * GROUP, 128, dtype=BF16)

    packed = (
        array(Y_ROWS, 128),
        array(Y_ROWS, 128),
        array(*tiles.shape, dtype=jnp.int32),
        array(*slots.shape, dtype=jnp.int32),
        held(EARLY),
    )
    scratch = [pltpu.SMEM((2, CAPY), jnp.int32), pltpu.SemaphoreType.DMA((3,))]
    sources = (side, tiles, slots, weights, held_rows, held_vel)
    back, *early = call(
        early_kernel,
        hbm(4) + vmem(2),
        (array(BACK_ROWS, 128),) + packed,
        scratch + [pltpu.SemaphoreType.DMA],
    )(*sources)
    lower = shift(back, "gx", -1)
    y1, y0, held_tiles, held_slots, late, second = call(
        late_kernel,
        hbm(4) + vmem(6),
        packed + (held(SECOND),),
        scratch + [pltpu.SemaphoreType.DMA] * 2,
    )(*sources, *early[:4])
    y1 = swap(y1, "gy", 1)
    y0 = swap(y0, "gy", 0)
    second, turned = call(
        fill_kernel,
        hbm() + vmem(3),
        (held(SECOND), array(EARLY * 256, 256, dtype=BF16)),
        [pltpu.SemaphoreType.DMA],
    )(weights, early[4], late, second)
    ry1, ry0 = call(relay_kernel, vmem(3), (array(R_ROWS, 128),) * 2, cost=300000000)(
        upper, lower, turned
    )
    ry1 = swap(ry1, "gy", 1)
    ry0 = swap(ry0, "gy", 0)
    lm, mm, strips, partial, picks, third = call(
        main_kernel,
        vmem(8) + hbm(),
        (
            array(NBD, 128),
            array(NBD, 128),
            array(3, EXT, 128),
            array(NBD, 512),
            array(NBD, POOL_DIAG, dtype=BF16),
            held(NBD // 8 - EARLY - SECOND),
        ),
        [
            pltpu.VMEM((3, LZ, EXT, 128), F32),
            pltpu.VMEM((15, LZ, EXT, 128), F32),
            pltpu.VMEM((2 * NBD, POOL), BF16),
            pltpu.VMEM((POOL, 256), BF16),
            pltpu.VMEM((2 * NBD, 256), F32),
            pltpu.SemaphoreType.DMA,
        ],
        cost=5000000,
    )(held_vel, upper, lower, y1, y0, held_rows, held_tiles, held_slots, weights)
    result = call(
        final_kernel,
        vmem(10),
        array(NBD, 128),
        [
            pltpu.VMEM((3, 1, EXT, 128), F32),
            pltpu.VMEM((15, 1, EXT, 128), F32),
            pltpu.VMEM((NBD, 128), F32),
            pltpu.VMEM((NBD, 128), F32),
            pltpu.VMEM((POOL_DIAG, 512), BF16),
            pltpu.VMEM((NBD, 512), F32),
            pltpu.VMEM((4 * NBD, 256), BF16),
            pltpu.VMEM((2, NBD, 128), F32),
        ],
    )(lm, mm, strips, ry1, ry0, partial, picks, turned, second, third)
    return result[None, None]


def solution(mesh):
    return jax.shard_map(
        on_device,
        mesh=mesh,
        in_specs=(
            P(None, "gx", None, "gy"),
            P("gx", "gy", None, None),
            P("gx", "gy", None),
            P("gx", "gy", None, None),
            P("gx", "gy", None, None),
            P("gx", "gy", None, None),
            P("gx", "gy", None, None),
            P("gx", "gy", None, None, None),
        ),
        out_specs=P("gx", "gy", None, None),
        check_vma=False,
    )
```

```python
import functools

import jax
import jax.numpy as jnp
from jax import lax
from jax.experimental import pallas as pl
from jax.experimental.pallas import tpu as pltpu
from jax.sharding import PartitionSpec as P

CX = 32
LZ = 4
NBD = 256
CAPX = 128
CAPY = 64
CAPD = 32

TIME_STEP = 0.5

VEL_AT = CAPD
DIAG1_AT = CAPD + 24
UP_AT = 2 * CAPD + 24
X_ROWS = UP_AT + CAPX
BACK_ROWS = 24
Y_ROWS = CAPY + CX
R_ROWS = CAPD + 8

POOL = NBD + CAPX + 2 * CAPY
POOL_DIAG = 128
UP_POOL = NBD
LOW_POOL = NBD + CAPX
HIGH_POOL = LOW_POOL + CAPY
DIAG_LOW_POOL = HIGH_POOL + CAPY
DIAG_HIGH_POOL = DIAG_LOW_POOL + CAPD

EXT = 48
GROUP = 8 * 64
EARLY = 10
SECOND = 6
F32 = jnp.float32
BF16 = jnp.bfloat16


def lanes_of(shape):
    return lax.broadcasted_iota(jnp.int32, shape, 1)


def roll_lanes(x, shift):
    shift = shift % 128
    return x if shift == 0 else pltpu.roll(x, shift, 1)


def odd(axis):
    return lax.rem(lax.axis_index(axis), 2) == 1


def pack_x_kernel(
    up_hbm, diag_hbm, rows_hbm, vel_hbm, ahead, rows, vel, up_list, diag_list, sems
):
    fetches = [
        pltpu.make_async_copy(source, target, sems.at[n])
        for n, (source, target) in enumerate(
            ((up_hbm, up_list), (diag_hbm, diag_list), (rows_hbm, rows), (vel_hbm, vel))
        )
    ]
    for fetch in fetches:
        fetch.start()
    for fetch in fetches[:3]:
        fetch.wait()
    for i in range(CAPD):
        ahead[i : i + 1, :] = rows[pl.ds(diag_list[0, i], 1), :]
        ahead[DIAG1_AT + i : DIAG1_AT + i + 1, :] = rows[pl.ds(diag_list[1, i], 1), :]
    for i in range(CAPX):
        ahead[UP_AT + i : UP_AT + i + 1, :] = rows[pl.ds(up_list[i], 1), :]
    fetches[3].wait()
    for c in range(3):
        ahead[VEL_AT + 8 * c : VEL_AT + 8 * c + 8, :] = vel[c * 128 + 120 : c * 128 + 128, :]


def weight_copy(weights, start, held, sem):
    return pltpu.make_async_copy(weights.at[pl.ds(start * GROUP, held.shape[0]), :], held, sem)


def pack_y(sources, outs, side_list, sems, weight_copies):
    side_hbm, tiles_hbm, slots_hbm, rows, vel = sources
    y1, y0, tiles, slots = outs
    is_odd = odd("gy")
    first = jnp.where(is_odd, 0, 1)
    fetches = [
        pltpu.make_async_copy(source, target, sems.at[n])
        for n, (source, target) in enumerate(
            ((side_hbm, side_list), (tiles_hbm, tiles), (slots_hbm, slots))
        )
    ]
    fetches += weight_copies
    for fetch in fetches:
        fetch.start()
    fetches[0].wait()
    for i in range(CAPY):
        y1[i : i + 1, :] = rows[pl.ds(side_list[first, i], 1), :]
        y0[i : i + 1, :] = rows[pl.ds(side_list[1 - first, i], 1), :]
    lane = lanes_of((8, 128))
    for xv in range(4):
        plus = jnp.zeros((8, 128), F32)
        minus = jnp.zeros((8, 128), F32)
        for z in range(LZ):
            for c in range(3):
                base = z * 32 + c * 8
                plane = vel[pl.ds(c * 128 + xv * 32 + z, 8, stride=4), :]
                here = (lane >= base) & (lane < base + 2)
                plus = jnp.where(here, roll_lanes(plane, base - 126), plus)
                minus = jnp.where(here, roll_lanes(plane, base), minus)
        at = CAPY + 8 * xv
        y1[at : at + 8, :] = jnp.where(is_odd, plus, minus)
        y0[at : at + 8, :] = jnp.where(is_odd, minus, plus)
    for fetch in fetches[1:]:
        fetch.wait()


def early_kernel(
    side, tiles_hbm, slots_hbm, weights, rows, vel, back, y1, y0, tiles, slots, held,
    side_list, sems, sem,
):
    for c in range(3):
        back[8 * c : 8 * c + 8, :] = vel[c * 128 : c * 128 + 8, :]

    @pl.when(lax.axis_index("gx") == 0)
    def _():
        sources = (side, tiles_hbm, slots_hbm, rows, vel)
        copies = [weight_copy(weights, 0, held, sem)]
        pack_y(sources, (y1, y0, tiles, slots), side_list, sems, copies)


def late_kernel(
    side, tiles_hbm, slots_hbm, weights, rows, vel, y1_early, y0_early, tiles_early, slots_early,
    y1, y0, tiles, slots, held, second, side_list, sems, sem, sem2,
):
    @pl.when(lax.axis_index("gx") == 0)
    def _():
        y1[...] = y1_early[...]
        y0[...] = y0_early[...]
        tiles[...] = tiles_early[...]
        slots[...] = slots_early[...]

    @pl.when(lax.axis_index("gx") != 0)
    def _():
        sources = (side, tiles_hbm, slots_hbm, rows, vel)
        copies = [
            weight_copy(weights, 0, held, sem),
            weight_copy(weights, EARLY, second, sem2),
        ]
        pack_y(sources, (y1, y0, tiles, slots), side_list, sems, copies)


def turn(held, turned):
    for n in range(2 * EARLY):
        turned[128 * n : 128 * n + 128, :] = jnp.transpose(held[256 * n : 256 * n + 256, :])


def fill_kernel(weights, held_early, held_late, second_late, second, turned, sem):
    copy = weight_copy(weights, EARLY, second, sem)

    @pl.when(lax.axis_index("gx") == 0)
    def _():
        copy.start()

        @after_start
        def _():
            turn(held_early, turned)

        copy.wait()

    @pl.when(lax.axis_index("gx") != 0)
    def _():
        second[...] = second_late[...]
        turn(held_late, turned)


def relay_kernel(upper, lower, _turned, ry1, ry0):
    y_odd = odd("gy")
    for i in range(0, CAPD, 8):
        plus, minus = upper[i : i + 8, :], upper[DIAG1_AT + i : DIAG1_AT + i + 8, :]
        ry1[i : i + 8, :] = jnp.where(y_odd, plus, minus)
        ry0[i : i + 8, :] = jnp.where(y_odd, minus, plus)
    lane = lanes_of((8, 128))
    plus = jnp.zeros((8, 128), F32)
    minus = jnp.zeros((8, 128), F32)
    for c in range(3):
        parts = (upper[VEL_AT + 8 * c : VEL_AT + 8 * c + 8, :], lower[8 * c : 8 * c + 8, :])
        for k, part in enumerate(parts):
            base = (2 * c + k) * 8
            here = (lane >= base) & (lane < base + 2)
            plus = jnp.where(here, roll_lanes(part, base - 126), plus)
            minus = jnp.where(here, roll_lanes(part, base), minus)
    ry1[CAPD:, :] = jnp.where(y_odd, plus, minus)
    ry0[CAPD:, :] = jnp.where(y_odd, minus, plus)


PAIRS = ((0, 0), (1, 1), (2, 2), (0, 1), (0, 2), (1, 2))


def plane_diff(f):
    last = len(f) - 1
    return [
        f[1] - f[0]
        if p == 0
        else f[last] - f[last - 1]
        if p == last
        else (f[p + 1] - f[p - 1]) * 0.5
        for p in range(last + 1)
    ]


def strip_diff(f):
    (f,) = f
    level = lanes_of(f.shape) // 32
    above, below = roll_lanes(f, -32), roll_lanes(f, 32)
    inner = (above - below) * 0.5
    return [jnp.where(level == 0, above - f, jnp.where(level == LZ - 1, f - below, inner))]


def strain(before, here, after, along_z):
    grad = [
        (
            (after[i] - before[i]) * 0.5,
            (roll_lanes(here[i], -1) - roll_lanes(here[i], 1)) * 0.5,
            along_z[i],
        )
        for i in range(3)
    ]
    rate = [grad[i][j] if i == j else 0.5 * (grad[i][j] + grad[j][i]) for i, j in PAIRS]
    own = rate[0] * rate[0] + rate[1] * rate[1] + rate[2] * rate[2]
    cross = rate[3] * rate[3] + rate[4] * rate[4] + rate[5] * rate[5]
    return rate, jnp.sqrt(2.0 * own + 4.0 * cross)


def filtered(before, here, after):
    across = 0.25 * (before + after) + 0.5 * here
    return 0.25 * (roll_lanes(across, 1) + roll_lanes(across, -1)) + 0.5 * across


def stencil(u, q, planes, diff, emit):
    for r in range(0, CX + 8, 8):
        here = [[u[c, p, r + 1 : r + 9, :] for p in range(planes)] for c in range(3)]
        along_z = [diff(here[c]) for c in range(3)]
        for p in range(planes):
            before = [u[c, p, r : r + 8, :] for c in range(3)]
            after = [u[c, p, r + 2 : r + 10, :] for c in range(3)]
            mid = [here[c][p] for c in range(3)]
            rate, size = strain(before, mid, after, [along_z[c][p] for c in range(3)])
            for n, (i, j) in enumerate(PAIRS):
                q[n, p, r : r + 8, :] = size * rate[n]
                q[6 + n, p, r : r + 8, :] = mid[i] * mid[j]
            for c in range(3):
                q[12 + c, p, r : r + 8, :] = filtered(before[c], mid[c], after[c])
    for r in range(0, CX, 8):
        here = [[q[12 + c, p, r + 1 : r + 9, :] for p in range(planes)] for c in range(3)]
        along_z = [diff(here[c]) for c in range(3)]
        for p in range(planes):
            before = [q[12 + c, p, r : r + 8, :] for c in range(3)]
            after = [q[12 + c, p, r + 2 : r + 10, :] for c in range(3)]
            mid = [here[c][p] for c in range(3)]
            rate, size = strain(before, mid, after, [along_z[c][p] for c in range(3)])
            size = 4.0 * size

            def smoothed(n):
                return filtered(
                    q[n, p, r : r + 8, :], q[n, p, r + 1 : r + 9, :], q[n, p, r + 2 : r + 10, :]
                )

            lm, mm = 0.0, 0.0
            for n, (i, j) in enumerate(PAIRS):
                model = 2.0 * (smoothed(n) - size * rate[n])
                leonard = smoothed(6 + n) - mid[i] * mid[j]
                weight = 1.0 if i == j else 2.0
                lm += weight * (leonard * model)
                mm += weight * (model * model)
            emit(p, r, lm, mm)


def after_start(body):
    pl.loop(0, jnp.where(lax.axis_index("gx") >= 0, 1, 0))(lambda _: body())


def candidates(pool, at, value):
    high = value.astype(BF16)
    size = value.shape[0]
    pool[at : at + size, 0:128] = high
    pool[at : at + size, 128:256] = (value - high.astype(F32)).astype(BF16)


def main_kernel(
    vel, upper, lower, y1, y0, rows, tiles, slots, weights,
    lm, mm, strips, partial, diag_picks, third,
    u, q, picks, pool, picked, sem,
):
    fetch = weight_copy(weights, EARLY + SECOND, third, sem)

    fetch.start()

    @after_start
    def _():
        y_odd = odd("gy")
        lane = lanes_of((8, 128))
        for c in range(3):
            for z in range(LZ):
                u[c, z, 0:2, :] = upper[pl.ds(VEL_AT + 8 * c + z, 2, stride=4), :]
                u[c, z, 2 : CX + 2, :] = vel[pl.ds(c * 128 + z, CX, stride=4), :]
                u[c, z, CX + 2 : CX + 4, :] = lower[pl.ds(8 * c + z, 2, stride=4), :]
        for c in range(3):
            for r in range(0, CX + 8, 8):
                strip = jnp.zeros((8, 128), F32)
                for z in range(LZ):
                    base = 32 * z
                    plane = u[c, z, r : r + 8, :]
                    left = (lane >= base + 2) & (lane < base + 6)
                    right = (lane >= base + 16) & (lane < base + 20)
                    strip = jnp.where(left, roll_lanes(plane, base + 2), strip)
                    strip = jnp.where(right, roll_lanes(plane, base + 16 - 124), strip)
                strips[c, r : r + 8, :] = strip
            for r in range(0, CX, 8):
                at = CAPY + r
                low = jnp.where(y_odd, y0[at : at + 8, :], y1[at : at + 8, :])
                high = jnp.where(y_odd, y1[at : at + 8, :], y0[at : at + 8, :])
                strip = strips[c, r + 2 : r + 10, :]
                strip = jnp.where(lane % 32 < 2, roll_lanes(low, -8 * c), strip)
                here = (lane % 32 >= 20) & (lane % 32 < 22)
                strip = jnp.where(here, roll_lanes(high, 20 - 8 * c), strip)
                strips[c, r + 2 : r + 10, :] = strip

        def emit(z, r, lm_part, mm_part):
            for k in range(2):
                lm[pl.ds(8 * r + 2 * z + k, 8, stride=8), :] = lm_part
                mm[pl.ds(8 * r + 2 * z + k, 8, stride=8), :] = mm_part

        stencil(u, q, LZ, plane_diff, emit)

        tile = tiles[...]
        starts = (0, UP_POOL, LOW_POOL, HIGH_POOL, DIAG_LOW_POOL, DIAG_HIGH_POOL)
        index = slots[...]
        for n, start in enumerate(starts):
            index = index + jnp.where(tile == n, start, 0)
        index = index.astype(F32)
        column = lanes_of((128, 128)).astype(F32)
        hits = []
        for k in range(2):
            for half in range(2):
                line = index[k : k + 1, half * 128 : half * 128 + 128]
                wanted = jnp.transpose(jnp.broadcast_to(line, (128, 128)))
                at = k * NBD + half * 128
                for part in range(POOL // 128):
                    hit = jnp.where(wanted == column + 128.0 * part, 1.0, 0.0)
                    picks[at : at + 128, part * 128 : part * 128 + 128] = hit.astype(BF16)
                hit = (wanted - (POOL - 64.0 * k)) == column
                mine = (column >= 64.0) if k else (column < 64.0)
                hits.append(jnp.where(hit & mine, 1.0, 0.0))
        for half in range(2):
            diag_picks[half * 128 : half * 128 + 128, :] = (hits[half] + hits[2 + half]).astype(BF16)
        candidates(pool, 0, rows[...])
        candidates(pool, UP_POOL, upper[UP_AT:, :])
        candidates(pool, LOW_POOL, jnp.where(y_odd, y0[:CAPY, :], y1[:CAPY, :]))
        candidates(pool, HIGH_POOL, jnp.where(y_odd, y1[:CAPY, :], y0[:CAPY, :]))
        picked[...] = jnp.dot(picks[...], pool[...], preferred_element_type=F32)
        front = lane < 64
        for r in range(0, NBD, 8):
            for n in range(2):
                first = picked[r : r + 8, 128 * n : 128 * n + 128]
                second = picked[NBD + r : NBD + r + 8, 128 * n : 128 * n + 128]
                partial[r : r + 8, 128 * n : 128 * n + 128] = jnp.where(
                    front, first, roll_lanes(second, 64)
                )
                partial[r : r + 8, 256 + 128 * n : 384 + 128 * n] = jnp.where(
                    front, roll_lanes(first, 64), second
                )

    fetch.wait()


def final_kernel(
    lm_in, mm_in, strips, ry1, ry0, partial, picks, turned, second, third, out,
    u, q, lm, mm, pool, picked, lefts, departs,
):
    y_odd = odd("gy")
    lane = lanes_of((8, 128))
    lm[...] = lm_in[...]
    mm[...] = mm_in[...]

    diag = jnp.concatenate(
        [
            jnp.where(y_odd, ry0[:CAPD, :], ry1[:CAPD, :]),
            jnp.where(y_odd, ry1[:CAPD, :], ry0[:CAPD, :]),
        ],
        axis=0,
    )
    high = diag.astype(BF16).astype(F32)
    front = lanes_of((2 * CAPD, 128)) < 64
    for n, term in enumerate((high, diag - high)):
        swapped = roll_lanes(term, 64)
        for at, value in (
            (128 * n, (jnp.where(front, term, 0.0), jnp.where(front, 0.0, swapped))),
            (256 + 128 * n, (jnp.where(front, swapped, 0.0), jnp.where(front, 0.0, term))),
        ):
            pool[: 2 * CAPD, at : at + 128] = value[0].astype(BF16)
            pool[2 * CAPD :, at : at + 128] = value[1].astype(BF16)
    picked[...] = partial[...] + jnp.dot(picks[...], pool[...], preferred_element_type=F32)

    low = jnp.where(y_odd, ry0[CAPD:, :], ry1[CAPD:, :])
    high = jnp.where(y_odd, ry1[CAPD:, :], ry0[CAPD:, :])
    u[...] = strips[...].reshape(u.shape)
    for c in range(3):
        for k, at in enumerate((0, CX + 2)):
            base = (2 * c + k) * 8
            for x in range(2):
                row = u[c, 0, at + x : at + x + 1, :]
                one = lanes_of((1, 128))
                for z in range(LZ):
                    line = low[4 * x + z : 4 * x + z + 1, :]
                    here = (one >= 32 * z) & (one < 32 * z + 2)
                    row = jnp.where(here, roll_lanes(line, 32 * z - base), row)
                    line = high[4 * x + z : 4 * x + z + 1, :]
                    here = (one >= 32 * z + 20) & (one < 32 * z + 22)
                    row = jnp.where(here, roll_lanes(line, 32 * z + 20 - base), row)
                u[c, 0, at + x : at + x + 1, :] = row

    def emit(_, r, lm_part, mm_part):
        for into, part in ((lm, lm_part), (mm, mm_part)):
            for z in range(LZ):
                left = roll_lanes(part, -(32 * z + 2))
                right = roll_lanes(part, 126 - (32 * z + 18))
                for k in range(2):
                    at = pl.ds(8 * r + 2 * z + k, 8, stride=8)
                    value = jnp.where(lane < 2, left, jnp.where(lane >= 126, right, into[at, :]))
                    into[at, :] = value

    stencil(u, q, 1, strip_diff, emit)

    row_of = lax.broadcasted_iota(jnp.int32, (8, 128), 0)
    top = lax.broadcasted_iota(jnp.int32, (16, 128), 0) % 8 < 4
    for x in range(CX):
        for n in range(2):
            left = jnp.concatenate(
                [
                    picked[8 * x : 8 * x + 8, 128 * n + at : 128 * n + at + 128]
                    for at in (0, 256)
                ],
                axis=0,
            )
            at = 32 * x + 16 * n
            lefts[at : at + 16, :128] = jnp.where(top, left, 0.0).astype(BF16)
            lefts[at : at + 16, 128:] = jnp.where(top, 0.0, left).astype(BF16)
    for x in range(CX):
        if x < EARLY:
            right, over = turned[256 * x : 256 * x + 256, :], 0
        else:
            late = x >= EARLY + SECOND
            held, at = (third, x - EARLY - SECOND) if late else (second, x - EARLY)
            at = GROUP * at
            right = jnp.concatenate([held[at : at + 256, :], held[at + 256 : at + 512, :]], axis=1)
            over = 1
        product = lax.dot_general(
            lefts[32 * x : 32 * x + 32, :],
            right,
            (((1,), (over,)), ((), ())),
            preferred_element_type=F32,
        )
        product = product[:16] + product[16:]
        for n in range(2):
            part = product[8 * n : 8 * n + 8, :]
            departs[n, 8 * x : 8 * x + 8, :] = jnp.where(
                row_of % 4 < 2, part[:, :128], part[:, 128:]
            )

    front = lane < 64
    even = row_of % 2 == 0
    for x in range(CX):
        lm_depart = departs[0, 8 * x : 8 * x + 8, :]
        mm_depart = departs[1, 8 * x : 8 * x + 8, :]
        lm_block, mm_block = lm[8 * x : 8 * x + 8, :], mm[8 * x : 8 * x + 8, :]
        ratio = (TIME_STEP / 1.5) * jnp.exp(0.125 * jnp.log(lm_depart * mm_depart))
        weight = ratio / (1.0 + ratio)
        lm_next = jnp.maximum(weight * lm_block + (1.0 - weight) * lm_depart, 0.0)
        mm_next = weight * mm_block + (1.0 - weight) * mm_depart
        lm_next = jnp.where(even, lm_next, roll_lanes(lm_next, 64))
        mm_next = jnp.where(even, roll_lanes(mm_next, 64), mm_next)
        out[8 * x : 8 * x + 8, :] = jnp.where(front, lm_next, mm_next)


def vmem(count=1):
    return [pl.BlockSpec(memory_space=pltpu.VMEM)] * count


def hbm(count=1):
    return [pl.BlockSpec(memory_space=pltpu.HBM)] * count


def array(*shape, dtype=F32):
    return jax.ShapeDtypeStruct(shape, dtype)


def call(kernel, ins, outs, scratch=(), cost=1000):
    return pl.pallas_call(
        kernel,
        in_specs=ins,
        out_specs=tuple(vmem(len(outs))) if isinstance(outs, tuple) else vmem()[0],
        out_shape=outs,
        scratch_shapes=list(scratch),
        compiler_params=pltpu.CompilerParams(vmem_limit_bytes=32 * 1024 * 1024),
        cost_estimate=pl.CostEstimate(flops=cost, bytes_accessed=cost, transcendentals=0),
    )


def swap(block, axis, start):
    count = lax.axis_size(axis)
    ahead = [(i, (i + 1) % count) for i in range(start, count, 2)]
    return lax.ppermute(block, axis, ahead + [(j, i) for i, j in ahead])


def shift(block, axis, distance):
    count = lax.axis_size(axis)
    return lax.ppermute(block, axis, [(i, (i + distance) % count) for i in range(count)])


def on_device(
    velocity, pair_blocks, send_up, send_side, send_diag, depart_tile, depart_slot, interp_weights
):
    def stay(x):
        return pltpu.with_memory_space_constraint(x, pltpu.HBM)

    vel = stay(velocity.reshape(3 * CX * LZ, 128))
    rows = stay(pair_blocks[0, 0])
    weights = stay(interp_weights.reshape(NBD * 64, 128))
    up, side, diag = stay(send_up[0, 0]), stay(send_side[0, 0]), stay(send_diag[0, 0])
    tiles, slots = stay(depart_tile[0, 0]), stay(depart_slot[0, 0])

    ahead, held_rows, held_vel = call(
        pack_x_kernel,
        hbm(4),
        (array(X_ROWS, 128), array(*rows.shape), array(*vel.shape)),
        [
            pltpu.SMEM((CAPX,), jnp.int32),
            pltpu.SMEM((2, CAPD), jnp.int32),
            pltpu.SemaphoreType.DMA((4,)),
        ],
    )(up, diag, rows, vel)
    upper = shift(ahead, "gx", 1)

    def held(count):
        return array(count * GROUP, 128, dtype=BF16)

    packed = (
        array(Y_ROWS, 128),
        array(Y_ROWS, 128),
        array(*tiles.shape, dtype=jnp.int32),
        array(*slots.shape, dtype=jnp.int32),
        held(EARLY),
    )
    scratch = [pltpu.SMEM((2, CAPY), jnp.int32), pltpu.SemaphoreType.DMA((3,))]
    sources = (side, tiles, slots, weights, held_rows, held_vel)
    back, *early = call(
        early_kernel,
        hbm(4) + vmem(2),
        (array(BACK_ROWS, 128),) + packed,
        scratch + [pltpu.SemaphoreType.DMA],
    )(*sources)
    lower = shift(back, "gx", -1)
    y1, y0, held_tiles, held_slots, late, second = call(
        late_kernel,
        hbm(4) + vmem(6),
        packed + (held(SECOND),),
        scratch + [pltpu.SemaphoreType.DMA] * 2,
    )(*sources, *early[:4])
    y1 = swap(y1, "gy", 1)
    y0 = swap(y0, "gy", 0)
    second, turned = call(
        fill_kernel,
        hbm() + vmem(3),
        (held(SECOND), array(EARLY * 256, 256, dtype=BF16)),
        [pltpu.SemaphoreType.DMA],
    )(weights, early[4], late, second)
    ry1, ry0 = call(relay_kernel, vmem(3), (array(R_ROWS, 128),) * 2, cost=300000000)(
        upper, lower, turned
    )
    ry1 = swap(ry1, "gy", 1)
    ry0 = swap(ry0, "gy", 0)
    lm, mm, strips, partial, picks, third = call(
        main_kernel,
        vmem(8) + hbm(),
        (
            array(NBD, 128),
            array(NBD, 128),
            array(3, EXT, 128),
            array(NBD, 512),
            array(NBD, POOL_DIAG, dtype=BF16),
            held(NBD // 8 - EARLY - SECOND),
        ),
        [
            pltpu.VMEM((3, LZ, EXT, 128), F32),
            pltpu.VMEM((15, LZ, EXT, 128), F32),
            pltpu.VMEM((2 * NBD, POOL), BF16),
            pltpu.VMEM((POOL, 256), BF16),
            pltpu.VMEM((2 * NBD, 256), F32),
            pltpu.SemaphoreType.DMA,
        ],
        cost=5000000,
    )(held_vel, upper, lower, y1, y0, held_rows, held_tiles, held_slots, weights)
    result = call(
        final_kernel,
        vmem(10),
        array(NBD, 128),
        [
            pltpu.VMEM((3, 1, EXT, 128), F32),
            pltpu.VMEM((15, 1, EXT, 128), F32),
            pltpu.VMEM((NBD, 128), F32),
            pltpu.VMEM((NBD, 128), F32),
            pltpu.VMEM((POOL_DIAG, 512), BF16),
            pltpu.VMEM((NBD, 512), F32),
            pltpu.VMEM((4 * NBD, 256), BF16),
            pltpu.VMEM((2, NBD, 128), F32),
        ],
    )(lm, mm, strips, ry1, ry0, partial, picks, turned, second, third)
    return result[None, None]


def solution(mesh):
    return jax.shard_map(
        on_device,
        mesh=mesh,
        in_specs=(
            P(None, "gx", None, "gy"),
            P("gx", "gy", None, None),
            P("gx", "gy", None),
            P("gx", "gy", None, None),
            P("gx", "gy", None, None),
            P("gx", "gy", None, None),
            P("gx", "gy", None, None),
            P("gx", "gy", None, None, None),
        ),
        out_specs=P("gx", "gy", None, None),
        check_vma=False,
    )
```

```python
import functools

import jax
import jax.numpy as jnp
from jax import lax
from jax.experimental import pallas as pl
from jax.experimental.pallas import tpu as pltpu
from jax.sharding import PartitionSpec as P

CX = 32
LZ = 4
NBD = 256
CAPX = 128
CAPY = 64
CAPD = 32

TIME_STEP = 0.5

VEL_AT = CAPD
DIAG1_AT = CAPD + 24
UP_AT = 2 * CAPD + 24
X_ROWS = UP_AT + CAPX
BACK_ROWS = 24
Y_ROWS = CAPY + CX
R_ROWS = CAPD + 8

POOL = NBD + CAPX + 2 * CAPY
POOL_DIAG = 128
UP_POOL = NBD
LOW_POOL = NBD + CAPX
HIGH_POOL = LOW_POOL + CAPY
DIAG_LOW_POOL = HIGH_POOL + CAPY
DIAG_HIGH_POOL = DIAG_LOW_POOL + CAPD

EXT = 48
GROUP = 8 * 64
EARLY = 8
SECOND = 8
F32 = jnp.float32
BF16 = jnp.bfloat16


def lanes_of(shape):
    return lax.broadcasted_iota(jnp.int32, shape, 1)


def roll_lanes(x, shift):
    shift = shift % 128
    return x if shift == 0 else pltpu.roll(x, shift, 1)


def odd(axis):
    return lax.rem(lax.axis_index(axis), 2) == 1


def pack_x_kernel(
    up_hbm, diag_hbm, rows_hbm, vel_hbm, ahead, rows, vel, up_list, diag_list, sems
):
    fetches = [
        pltpu.make_async_copy(source, target, sems.at[n])
        for n, (source, target) in enumerate(
            ((up_hbm, up_list), (diag_hbm, diag_list), (rows_hbm, rows), (vel_hbm, vel))
        )
    ]
    for fetch in fetches:
        fetch.start()
    for fetch in fetches[:3]:
        fetch.wait()
    for i in range(CAPD):
        ahead[i : i + 1, :] = rows[pl.ds(diag_list[0, i], 1), :]
        ahead[DIAG1_AT + i : DIAG1_AT + i + 1, :] = rows[pl.ds(diag_list[1, i], 1), :]
    for i in range(CAPX):
        ahead[UP_AT + i : UP_AT + i + 1, :] = rows[pl.ds(up_list[i], 1), :]
    fetches[3].wait()
    for c in range(3):
        ahead[VEL_AT + 8 * c : VEL_AT + 8 * c + 8, :] = vel[c * 128 + 120 : c * 128 + 128, :]


def weight_copy(weights, start, held, sem):
    return pltpu.make_async_copy(weights.at[pl.ds(start * GROUP, held.shape[0]), :], held, sem)


def pack_y(sources, outs, side_list, sems, weight_copies):
    side_hbm, tiles_hbm, slots_hbm, rows, vel = sources
    y1, y0, tiles, slots = outs
    is_odd = odd("gy")
    first = jnp.where(is_odd, 0, 1)
    fetches = [
        pltpu.make_async_copy(source, target, sems.at[n])
        for n, (source, target) in enumerate(
            ((side_hbm, side_list), (tiles_hbm, tiles), (slots_hbm, slots))
        )
    ]
    fetches += weight_copies
    for fetch in fetches:
        fetch.start()
    fetches[0].wait()
    for i in range(CAPY):
        y1[i : i + 1, :] = rows[pl.ds(side_list[first, i], 1), :]
        y0[i : i + 1, :] = rows[pl.ds(side_list[1 - first, i], 1), :]
    lane = lanes_of((8, 128))
    for xv in range(4):
        plus = jnp.zeros((8, 128), F32)
        minus = jnp.zeros((8, 128), F32)
        for z in range(LZ):
            for c in range(3):
                base = z * 32 + c * 8
                plane = vel[pl.ds(c * 128 + xv * 32 + z, 8, stride=4), :]
                here = (lane >= base) & (lane < base + 2)
                plus = jnp.where(here, roll_lanes(plane, base - 126), plus)
                minus = jnp.where(here, roll_lanes(plane, base), minus)
        at = CAPY + 8 * xv
        y1[at : at + 8, :] = jnp.where(is_odd, plus, minus)
        y0[at : at + 8, :] = jnp.where(is_odd, minus, plus)
    for fetch in fetches[1:]:
        fetch.wait()


def early_kernel(
    side, tiles_hbm, slots_hbm, weights, rows, vel, back, y1, y0, tiles, slots, held,
    side_list, sems, sem,
):
    for c in range(3):
        back[8 * c : 8 * c + 8, :] = vel[c * 128 : c * 128 + 8, :]

    @pl.when(lax.axis_index("gx") == 0)
    def _():
        sources = (side, tiles_hbm, slots_hbm, rows, vel)
        copies = [weight_copy(weights, 0, held, sem)]
        pack_y(sources, (y1, y0, tiles, slots), side_list, sems, copies)


def late_kernel(
    side, tiles_hbm, slots_hbm, weights, rows, vel, y1_early, y0_early, tiles_early, slots_early,
    y1, y0, tiles, slots, held, second, side_list, sems, sem, sem2,
):
    @pl.when(lax.axis_index("gx") == 0)
    def _():
        y1[...] = y1_early[...]
        y0[...] = y0_early[...]
        tiles[...] = tiles_early[...]
        slots[...] = slots_early[...]

    @pl.when(lax.axis_index("gx") != 0)
    def _():
        sources = (side, tiles_hbm, slots_hbm, rows, vel)
        copies = [
            weight_copy(weights, 0, held, sem),
            weight_copy(weights, EARLY, second, sem2),
        ]
        pack_y(sources, (y1, y0, tiles, slots), side_list, sems, copies)


def turn(held, turned):
    for n in range(2 * EARLY):
        turned[128 * n : 128 * n + 128, :] = jnp.transpose(held[256 * n : 256 * n + 256, :])


def fill_kernel(weights, held_early, held_late, second_late, second, turned, sem):
    copy = weight_copy(weights, EARLY, second, sem)

    @pl.when(lax.axis_index("gx") == 0)
    def _():
        copy.start()

        @after_start
        def _():
            turn(held_early, turned)

        copy.wait()

    @pl.when(lax.axis_index("gx") != 0)
    def _():
        second[...] = second_late[...]
        turn(held_late, turned)


def relay_kernel(upper, lower, _turned, ry1, ry0):
    y_odd = odd("gy")
    for i in range(0, CAPD, 8):
        plus, minus = upper[i : i + 8, :], upper[DIAG1_AT + i : DIAG1_AT + i + 8, :]
        ry1[i : i + 8, :] = jnp.where(y_odd, plus, minus)
        ry0[i : i + 8, :] = jnp.where(y_odd, minus, plus)
    lane = lanes_of((8, 128))
    plus = jnp.zeros((8, 128), F32)
    minus = jnp.zeros((8, 128), F32)
    for c in range(3):
        parts = (upper[VEL_AT + 8 * c : VEL_AT + 8 * c + 8, :], lower[8 * c : 8 * c + 8, :])
        for k, part in enumerate(parts):
            base = (2 * c + k) * 8
            here = (lane >= base) & (lane < base + 2)
            plus = jnp.where(here, roll_lanes(part, base - 126), plus)
            minus = jnp.where(here, roll_lanes(part, base), minus)
    ry1[CAPD:, :] = jnp.where(y_odd, plus, minus)
    ry0[CAPD:, :] = jnp.where(y_odd, minus, plus)


PAIRS = ((0, 0), (1, 1), (2, 2), (0, 1), (0, 2), (1, 2))


def plane_diff(f):
    last = len(f) - 1
    return [
        f[1] - f[0]
        if p == 0
        else f[last] - f[last - 1]
        if p == last
        else (f[p + 1] - f[p - 1]) * 0.5
        for p in range(last + 1)
    ]


def strip_diff(f):
    (f,) = f
    level = lanes_of(f.shape) // 32
    above, below = roll_lanes(f, -32), roll_lanes(f, 32)
    inner = (above - below) * 0.5
    return [jnp.where(level == 0, above - f, jnp.where(level == LZ - 1, f - below, inner))]


def strain(before, here, after, along_z):
    grad = [
        (
            (after[i] - before[i]) * 0.5,
            (roll_lanes(here[i], -1) - roll_lanes(here[i], 1)) * 0.5,
            along_z[i],
        )
        for i in range(3)
    ]
    rate = [grad[i][j] if i == j else 0.5 * (grad[i][j] + grad[j][i]) for i, j in PAIRS]
    own = rate[0] * rate[0] + rate[1] * rate[1] + rate[2] * rate[2]
    cross = rate[3] * rate[3] + rate[4] * rate[4] + rate[5] * rate[5]
    return rate, jnp.sqrt(2.0 * own + 4.0 * cross)


def filtered(before, here, after):
    across = 0.25 * (before + after) + 0.5 * here
    return 0.25 * (roll_lanes(across, 1) + roll_lanes(across, -1)) + 0.5 * across


def stencil(u, q, planes, diff, emit):
    for r in range(0, CX + 8, 8):
        here = [[u[c, p, r + 1 : r + 9, :] for p in range(planes)] for c in range(3)]
        along_z = [diff(here[c]) for c in range(3)]
        for p in range(planes):
            before = [u[c, p, r : r + 8, :] for c in range(3)]
            after = [u[c, p, r + 2 : r + 10, :] for c in range(3)]
            mid = [here[c][p] for c in range(3)]
            rate, size = strain(before, mid, after, [along_z[c][p] for c in range(3)])
            for n, (i, j) in enumerate(PAIRS):
                q[n, p, r : r + 8, :] = size * rate[n]
                q[6 + n, p, r : r + 8, :] = mid[i] * mid[j]
            for c in range(3):
                q[12 + c, p, r : r + 8, :] = filtered(before[c], mid[c], after[c])
    for r in range(0, CX, 8):
        here = [[q[12 + c, p, r + 1 : r + 9, :] for p in range(planes)] for c in range(3)]
        along_z = [diff(here[c]) for c in range(3)]
        for p in range(planes):
            before = [q[12 + c, p, r : r + 8, :] for c in range(3)]
            after = [q[12 + c, p, r + 2 : r + 10, :] for c in range(3)]
            mid = [here[c][p] for c in range(3)]
            rate, size = strain(before, mid, after, [along_z[c][p] for c in range(3)])
            size = 4.0 * size

            def smoothed(n):
                return filtered(
                    q[n, p, r : r + 8, :], q[n, p, r + 1 : r + 9, :], q[n, p, r + 2 : r + 10, :]
                )

            lm, mm = 0.0, 0.0
            for n, (i, j) in enumerate(PAIRS):
                model = 2.0 * (smoothed(n) - size * rate[n])
                leonard = smoothed(6 + n) - mid[i] * mid[j]
                weight = 1.0 if i == j else 2.0
                lm += weight * (leonard * model)
                mm += weight * (model * model)
            emit(p, r, lm, mm)


def after_start(body):
    pl.loop(0, jnp.where(lax.axis_index("gx") >= 0, 1, 0))(lambda _: body())


def candidates(pool, at, value):
    high = value.astype(BF16)
    size = value.shape[0]
    pool[at : at + size, 0:128] = high
    pool[at : at + size, 128:256] = (value - high.astype(F32)).astype(BF16)


def main_kernel(
    vel, upper, lower, y1, y0, rows, tiles, slots, weights,
    lm, mm, strips, partial, diag_picks, third,
    u, q, picks, pool, picked, sem,
):
    fetch = weight_copy(weights, EARLY + SECOND, third, sem)

    fetch.start()

    @after_start
    def _():
        y_odd = odd("gy")
        lane = lanes_of((8, 128))
        for c in range(3):
            for z in range(LZ):
                u[c, z, 0:2, :] = upper[pl.ds(VEL_AT + 8 * c + z, 2, stride=4), :]
                u[c, z, 2 : CX + 2, :] = vel[pl.ds(c * 128 + z, CX, stride=4), :]
                u[c, z, CX + 2 : CX + 4, :] = lower[pl.ds(8 * c + z, 2, stride=4), :]
        for c in range(3):
            for r in range(0, CX + 8, 8):
                strip = jnp.zeros((8, 128), F32)
                for z in range(LZ):
                    base = 32 * z
                    plane = u[c, z, r : r + 8, :]
                    left = (lane >= base + 2) & (lane < base + 6)
                    right = (lane >= base + 16) & (lane < base + 20)
                    strip = jnp.where(left, roll_lanes(plane, base + 2), strip)
                    strip = jnp.where(right, roll_lanes(plane, base + 16 - 124), strip)
                strips[c, r : r + 8, :] = strip
            for r in range(0, CX, 8):
                at = CAPY + r
                low = jnp.where(y_odd, y0[at : at + 8, :], y1[at : at + 8, :])
                high = jnp.where(y_odd, y1[at : at + 8, :], y0[at : at + 8, :])
                strip = strips[c, r + 2 : r + 10, :]
                strip = jnp.where(lane % 32 < 2, roll_lanes(low, -8 * c), strip)
                here = (lane % 32 >= 20) & (lane % 32 < 22)
                strip = jnp.where(here, roll_lanes(high, 20 - 8 * c), strip)
                strips[c, r + 2 : r + 10, :] = strip

        def emit(z, r, lm_part, mm_part):
            for k in range(2):
                lm[pl.ds(8 * r + 2 * z + k, 8, stride=8), :] = lm_part
                mm[pl.ds(8 * r + 2 * z + k, 8, stride=8), :] = mm_part

        stencil(u, q, LZ, plane_diff, emit)

        tile = tiles[...]
        starts = (0, UP_POOL, LOW_POOL, HIGH_POOL, DIAG_LOW_POOL, DIAG_HIGH_POOL)
        index = slots[...]
        for n, start in enumerate(starts):
            index = index + jnp.where(tile == n, start, 0)
        index = index.astype(F32)
        column = lanes_of((128, 128)).astype(F32)
        hits = []
        for k in range(2):
            for half in range(2):
                line = index[k : k + 1, half * 128 : half * 128 + 128]
                wanted = jnp.transpose(jnp.broadcast_to(line, (128, 128)))
                at = k * NBD + half * 128
                for part in range(POOL // 128):
                    hit = jnp.where(wanted == column + 128.0 * part, 1.0, 0.0)
                    picks[at : at + 128, part * 128 : part * 128 + 128] = hit.astype(BF16)
                hit = (wanted - (POOL - 64.0 * k)) == column
                mine = (column >= 64.0) if k else (column < 64.0)
                hits.append(jnp.where(hit & mine, 1.0, 0.0))
        for half in range(2):
            diag_picks[half * 128 : half * 128 + 128, :] = (hits[half] + hits[2 + half]).astype(BF16)
        candidates(pool, 0, rows[...])
        candidates(pool, UP_POOL, upper[UP_AT:, :])
        candidates(pool, LOW_POOL, jnp.where(y_odd, y0[:CAPY, :], y1[:CAPY, :]))
        candidates(pool, HIGH_POOL, jnp.where(y_odd, y1[:CAPY, :], y0[:CAPY, :]))
        picked[...] = jnp.dot(picks[...], pool[...], preferred_element_type=F32)
        front = lane < 64
        for r in range(0, NBD, 8):
            for n in range(2):
                first = picked[r : r + 8, 128 * n : 128 * n + 128]
                second = picked[NBD + r : NBD + r + 8, 128 * n : 128 * n + 128]
                partial[r : r + 8, 128 * n : 128 * n + 128] = jnp.where(
                    front, first, roll_lanes(second, 64)
                )
                partial[r : r + 8, 256 + 128 * n : 384 + 128 * n] = jnp.where(
                    front, roll_lanes(first, 64), second
                )

    fetch.wait()


def final_kernel(
    lm_in, mm_in, strips, ry1, ry0, partial, picks, turned, second, third, out,
    u, q, lm, mm, pool, picked, lefts, departs,
):
    y_odd = odd("gy")
    lane = lanes_of((8, 128))
    lm[...] = lm_in[...]
    mm[...] = mm_in[...]

    diag = jnp.concatenate(
        [
            jnp.where(y_odd, ry0[:CAPD, :], ry1[:CAPD, :]),
            jnp.where(y_odd, ry1[:CAPD, :], ry0[:CAPD, :]),
        ],
        axis=0,
    )
    high = diag.astype(BF16).astype(F32)
    front = lanes_of((2 * CAPD, 128)) < 64
    for n, term in enumerate((high, diag - high)):
        swapped = roll_lanes(term, 64)
        for at, value in (
            (128 * n, (jnp.where(front, term, 0.0), jnp.where(front, 0.0, swapped))),
            (256 + 128 * n, (jnp.where(front, swapped, 0.0), jnp.where(front, 0.0, term))),
        ):
            pool[: 2 * CAPD, at : at + 128] = value[0].astype(BF16)
            pool[2 * CAPD :, at : at + 128] = value[1].astype(BF16)
    picked[...] = partial[...] + jnp.dot(picks[...], pool[...], preferred_element_type=F32)

    low = jnp.where(y_odd, ry0[CAPD:, :], ry1[CAPD:, :])
    high = jnp.where(y_odd, ry1[CAPD:, :], ry0[CAPD:, :])
    u[...] = strips[...].reshape(u.shape)
    for c in range(3):
        for k, at in enumerate((0, CX + 2)):
            base = (2 * c + k) * 8
            for x in range(2):
                row = u[c, 0, at + x : at + x + 1, :]
                one = lanes_of((1, 128))
                for z in range(LZ):
                    line = low[4 * x + z : 4 * x + z + 1, :]
                    here = (one >= 32 * z) & (one < 32 * z + 2)
                    row = jnp.where(here, roll_lanes(line, 32 * z - base), row)
                    line = high[4 * x + z : 4 * x + z + 1, :]
                    here = (one >= 32 * z + 20) & (one < 32 * z + 22)
                    row = jnp.where(here, roll_lanes(line, 32 * z + 20 - base), row)
                u[c, 0, at + x : at + x + 1, :] = row

    def emit(_, r, lm_part, mm_part):
        for into, part in ((lm, lm_part), (mm, mm_part)):
            for z in range(LZ):
                left = roll_lanes(part, -(32 * z + 2))
                right = roll_lanes(part, 126 - (32 * z + 18))
                for k in range(2):
                    at = pl.ds(8 * r + 2 * z + k, 8, stride=8)
                    value = jnp.where(lane < 2, left, jnp.where(lane >= 126, right, into[at, :]))
                    into[at, :] = value

    stencil(u, q, 1, strip_diff, emit)

    row_of = lax.broadcasted_iota(jnp.int32, (8, 128), 0)
    top = lax.broadcasted_iota(jnp.int32, (16, 128), 0) % 8 < 4
    for x in range(CX):
        for n in range(2):
            left = jnp.concatenate(
                [
                    picked[8 * x : 8 * x + 8, 128 * n + at : 128 * n + at + 128]
                    for at in (0, 256)
                ],
                axis=0,
            )
            at = 32 * x + 16 * n
            lefts[at : at + 16, :128] = jnp.where(top, left, 0.0).astype(BF16)
            lefts[at : at + 16, 128:] = jnp.where(top, 0.0, left).astype(BF16)
    for x in range(CX):
        if x < EARLY:
            right, over = turned[256 * x : 256 * x + 256, :], 0
        else:
            late = x >= EARLY + SECOND
            held, at = (third, x - EARLY - SECOND) if late else (second, x - EARLY)
            at = GROUP * at
            right = jnp.concatenate([held[at : at + 256, :], held[at + 256 : at + 512, :]], axis=1)
            over = 1
        product = lax.dot_general(
            lefts[32 * x : 32 * x + 32, :],
            right,
            (((1,), (over,)), ((), ())),
            preferred_element_type=F32,
        )
        product = product[:16] + product[16:]
        for n in range(2):
            part = product[8 * n : 8 * n + 8, :]
            departs[n, 8 * x : 8 * x + 8, :] = jnp.where(
                row_of % 4 < 2, part[:, :128], part[:, 128:]
            )

    front = lane < 64
    even = row_of % 2 == 0
    for x in range(CX):
        lm_depart = departs[0, 8 * x : 8 * x + 8, :]
        mm_depart = departs[1, 8 * x : 8 * x + 8, :]
        lm_block, mm_block = lm[8 * x : 8 * x + 8, :], mm[8 * x : 8 * x + 8, :]
        ratio = (TIME_STEP / 1.5) * jnp.exp(0.125 * jnp.log(lm_depart * mm_depart))
        weight = ratio / (1.0 + ratio)
        lm_next = jnp.maximum(weight * lm_block + (1.0 - weight) * lm_depart, 0.0)
        mm_next = weight * mm_block + (1.0 - weight) * mm_depart
        lm_next = jnp.where(even, lm_next, roll_lanes(lm_next, 64))
        mm_next = jnp.where(even, roll_lanes(mm_next, 64), mm_next)
        out[8 * x : 8 * x + 8, :] = jnp.where(front, lm_next, mm_next)


def vmem(count=1):
    return [pl.BlockSpec(memory_space=pltpu.VMEM)] * count


def hbm(count=1):
    return [pl.BlockSpec(memory_space=pltpu.HBM)] * count


def array(*shape, dtype=F32):
    return jax.ShapeDtypeStruct(shape, dtype)


def call(kernel, ins, outs, scratch=(), cost=1000):
    return pl.pallas_call(
        kernel,
        in_specs=ins,
        out_specs=tuple(vmem(len(outs))) if isinstance(outs, tuple) else vmem()[0],
        out_shape=outs,
        scratch_shapes=list(scratch),
        compiler_params=pltpu.CompilerParams(vmem_limit_bytes=32 * 1024 * 1024),
        cost_estimate=pl.CostEstimate(flops=cost, bytes_accessed=cost, transcendentals=0),
    )


def swap(block, axis, start):
    count = lax.axis_size(axis)
    ahead = [(i, (i + 1) % count) for i in range(start, count, 2)]
    return lax.ppermute(block, axis, ahead + [(j, i) for i, j in ahead])


def shift(block, axis, distance):
    count = lax.axis_size(axis)
    return lax.ppermute(block, axis, [(i, (i + distance) % count) for i in range(count)])


def on_device(
    velocity, pair_blocks, send_up, send_side, send_diag, depart_tile, depart_slot, interp_weights
):
    def stay(x):
        return pltpu.with_memory_space_constraint(x, pltpu.HBM)

    vel = stay(velocity.reshape(3 * CX * LZ, 128))
    rows = stay(pair_blocks[0, 0])
    weights = stay(interp_weights.reshape(NBD * 64, 128))
    up, side, diag = stay(send_up[0, 0]), stay(send_side[0, 0]), stay(send_diag[0, 0])
    tiles, slots = stay(depart_tile[0, 0]), stay(depart_slot[0, 0])

    ahead, held_rows, held_vel = call(
        pack_x_kernel,
        hbm(4),
        (array(X_ROWS, 128), array(*rows.shape), array(*vel.shape)),
        [
            pltpu.SMEM((CAPX,), jnp.int32),
            pltpu.SMEM((2, CAPD), jnp.int32),
            pltpu.SemaphoreType.DMA((4,)),
        ],
    )(up, diag, rows, vel)
    upper = shift(ahead, "gx", 1)

    def held(count):
        return array(count * GROUP, 128, dtype=BF16)

    packed = (
        array(Y_ROWS, 128),
        array(Y_ROWS, 128),
        array(*tiles.shape, dtype=jnp.int32),
        array(*slots.shape, dtype=jnp.int32),
        held(EARLY),
    )
    scratch = [pltpu.SMEM((2, CAPY), jnp.int32), pltpu.SemaphoreType.DMA((3,))]
    sources = (side, tiles, slots, weights, held_rows, held_vel)
    back, *early = call(
        early_kernel,
        hbm(4) + vmem(2),
        (array(BACK_ROWS, 128),) + packed,
        scratch + [pltpu.SemaphoreType.DMA],
    )(*sources)
    lower = shift(back, "gx", -1)
    y1, y0, held_tiles, held_slots, late, second = call(
        late_kernel,
        hbm(4) + vmem(6),
        packed + (held(SECOND),),
        scratch + [pltpu.SemaphoreType.DMA] * 2,
    )(*sources, *early[:4])
    y1 = swap(y1, "gy", 1)
    y0 = swap(y0, "gy", 0)
    second, turned = call(
        fill_kernel,
        hbm() + vmem(3),
        (held(SECOND), array(EARLY * 256, 256, dtype=BF16)),
        [pltpu.SemaphoreType.DMA],
    )(weights, early[4], late, second)
    ry1, ry0 = call(relay_kernel, vmem(3), (array(R_ROWS, 128),) * 2, cost=300000000)(
        upper, lower, turned
    )
    ry1 = swap(ry1, "gy", 1)
    ry0 = swap(ry0, "gy", 0)
    lm, mm, strips, partial, picks, third = call(
        main_kernel,
        vmem(8) + hbm(),
        (
            array(NBD, 128),
            array(NBD, 128),
            array(3, EXT, 128),
            array(NBD, 512),
            array(NBD, POOL_DIAG, dtype=BF16),
            held(NBD // 8 - EARLY - SECOND),
        ),
        [
            pltpu.VMEM((3, LZ, EXT, 128), F32),
            pltpu.VMEM((15, LZ, EXT, 128), F32),
            pltpu.VMEM((2 * NBD, POOL), BF16),
            pltpu.VMEM((POOL, 256), BF16),
            pltpu.VMEM((2 * NBD, 256), F32),
            pltpu.SemaphoreType.DMA,
        ],
        cost=5000000,
    )(held_vel, upper, lower, y1, y0, held_rows, held_tiles, held_slots, weights)
    result = call(
        final_kernel,
        vmem(10),
        array(NBD, 128),
        [
            pltpu.VMEM((3, 1, EXT, 128), F32),
            pltpu.VMEM((15, 1, EXT, 128), F32),
            pltpu.VMEM((NBD, 128), F32),
            pltpu.VMEM((NBD, 128), F32),
            pltpu.VMEM((POOL_DIAG, 512), BF16),
            pltpu.VMEM((NBD, 512), F32),
            pltpu.VMEM((4 * NBD, 256), BF16),
            pltpu.VMEM((2, NBD, 128), F32),
        ],
    )(lm, mm, strips, ry1, ry0, partial, picks, turned, second, third)
    return result[None, None]


def solution(mesh):
    return jax.shard_map(
        on_device,
        mesh=mesh,
        in_specs=(
            P(None, "gx", None, "gy"),
            P("gx", "gy", None, None),
            P("gx", "gy", None),
            P("gx", "gy", None, None),
            P("gx", "gy", None, None),
            P("gx", "gy", None, None),
            P("gx", "gy", None, None),
            P("gx", "gy", None, None, None),
        ),
        out_specs=P("gx", "gy", None, None),
        check_vma=False,
    )
```
